768 devices in a mesh: dp: 12 (over z), fold: 4 (over x), tensor: 16 (over y, core).
Axes of the slice: x: 4, y: 8, z: 12, core: 2. Of those that a mesh axis runs over, the one named last changes fastest.
Arguments:
- attn_heads: bfloat16 [24576, 4096], P(('dp', 'fold'), 'tensor'), may hold values from -6 to 6
- w_out: bfloat16 [4096, 2048], P('tensor'), may hold values from -0.09375 to 0.09375
- residual: bfloat16 [24576, 2048], P(('dp', 'fold', 'tensor')), may hold values from -6 to 6
- gain_moe: float32 [2048], replicated, may hold values from 0.25 to 1.75
- router: bfloat16 [2048, 64], replicated, may hold values from -0.125 to 0.125
- route_ids: int32 [24576, 8], P(('dp', 'fold', 'tensor')), may hold values from 0 to 63, all different within a row; in each aligned block of 32 rows (0 to 31, 32 to 63, ...) at most 6 rows name the same one
- w_gate: bfloat16 [64, 2048, 768], P(('fold', 'tensor')), may hold values from -0.125 to 0.125
- w_up: bfloat16 [64, 2048, 768], P(('fold', 'tensor')), may hold values from -0.125 to 0.125
- w_down: bfloat16 [64, 768, 2048], P(('fold', 'tensor')), may hold values from -0.21875 to 0.21875
- bias: float32 [64], replicated, may hold values from -1 to 1
- gain_next: float32 [2048], replicated, may hold values from 0.25 to 1.75
- w_query: bfloat16 [2048, 4096], P(None, 'tensor'), may hold values from -0.125 to 0.125
Outputs:
- stream_out: bfloat16 [24576, 2048], P(('dp', 'fold', 'tensor'))
- query: bfloat16 [24576, 4096], P(('dp', 'fold'), 'tensor')
- new_bias: float32 [64], replicated
The draws below stay inside these ranges and needn't reach their ends.
Inputs may be any that keep to these rules, and one draw needn't show every extreme that they name: `route_ids`: each row names 8 different experts; among the rows of one device no expert is named by more than 6 rows.
All inputs are finite; a program needn't handle non-finite values.
Results may differ from the reference program's by a relative error of at most 0.006.
Values may be sent and summed in bfloat16 or wider, within the bound.
A program may use at most 64 MiB of HBM per device.

```python
import math
import jax
import jax.numpy as jnp
import numpy as np
from jax import lax

D = 2048
FF = 768
HEADS = 32
HD = 128
TOPK = 8
TOK_DEV = 32
EXPERTS = 64
CAP = 6
TOKENS = 24576
N_DP = 12
N_FOLD = 4
N_TENSOR = 16


def block_levels(key, shape, split, smallest, top_value):
    factor_of = 1.0
    for axis_at, parts in split:
        heights = jax.random.uniform(jax.random.fold_in(jax.random.fold_in(key, 6), axis_at), (parts,), jnp.float32, smallest / len(split), top_value / len(split))
        factor_of = factor_of * jnp.repeat(jnp.exp(heights), shape[axis_at] // parts).reshape((-1,) + (1,) * (len(shape) - 1 - axis_at))
    return factor_of


def routed_block(rng, own, number, rows, count, top, bound, skew):
    ranking = jax.random.permutation(rng, count)
    heavy_load, common = portions_of(count, rows * top, bound, skew, True), portions_of(count, rows * top, bound, skew, False)
    places = jnp.arange(count)

    def named(lengths, rotation):
        used = int((lengths > 0).sum())
        fixed = max(1, used // 4)
        shifted = fixed + (places - fixed + rotation * (used - fixed)) % max(1, count - fixed)
        return jnp.zeros((count,), jnp.int32).at[ranking[jnp.where(places < fixed, places, shifted)]].set(jnp.asarray(lengths, jnp.int32))

    lengths = jnp.where(number % 4 == 0, named(heavy_load, number // 4), named(common, number - number // 4 - 1))
    mixed = jax.random.permutation(jax.random.fold_in(own, 3), count)
    source_of, receiver = mixed[0:count // 2 * 2:2], mixed[1:count // 2 * 2:2]
    slack = jnp.minimum(lengths[source_of] - 1, bound - lengths[receiver]) // 2
    slack = jnp.where((source_of == ranking[0]) | (receiver == ranking[0]) | (lengths[receiver] == 0), 0, jnp.maximum(slack, 0))
    shifted = jax.random.randint(jax.random.fold_in(own, 4), (count // 2,), 0, 1 << 20) % (slack + 1)
    lengths = lengths.at[source_of].add(-shifted).at[receiver].add(shifted)
    members = jnp.searchsorted(jnp.cumsum(lengths), jnp.arange(rows * top), side="right").astype(jnp.int32)
    table = members.reshape(top, rows).T
    table = table[jax.random.permutation(jax.random.fold_in(own, 1), rows)]
    rotation = jax.random.randint(jax.random.fold_in(own, 2), (rows, 1), 0, top)
    return jnp.take_along_axis(table, (jnp.arange(top)[None, :] + rotation) % top, axis=1)


def portions_of(amount, total, bound, slope, full):
    loads = [(1 << 20) // math.isqrt(standing ** slope) + 1 for standing in range(1, amount + 1)]
    largest = bound if full else min(bound, max(-(-total // amount), total * loads[0] // sum(loads)))
    least = 1 if total - largest >= amount - 1 else 0
    holding, spare = [largest] + [least] * (amount - 1), total - largest - least * (amount - 1)
    while spare > 0:
        free = [i for i in range(1, amount) if holding[i] < largest] or [i for i in range(1, amount) if holding[i] < bound]
        mass, budget = sum([loads[i] for i in free]), spare
        for i in free:
            extra = min(bound - holding[i], max(1, budget * loads[i] // mass), spare)
            holding[i] = holding[i] + extra
            spare = spare - extra
    return np.array(holding)


def scatter_about(own_key, dims, width, bound, split=(), kind=jnp.bfloat16):
    entries = width * jax.random.normal(own_key, dims, jnp.float32)
    if split:
        entries = entries * block_levels(own_key, dims, split, -0.22, 0.18)
    return jnp.clip(entries, -bound, bound).astype(kind)


def setup_inputs(seed: int = 0) -> dict:
    arg_keys = jax.random.split(jax.random.key(seed), 13)
    attn_heads = scatter_about(arg_keys[0], (TOKENS, HEADS * HD), 1.0, 6.0, ((0, 48), (1, 16)))
    w_out = scatter_about(arg_keys[1], (HEADS * HD, D), (HEADS * HD) ** -0.5, 0.09375, ((0, 16),))
    residual = scatter_about(arg_keys[2], (TOKENS, D), 1.0, 6.0, ((0, 768),))
    gain_moe = jnp.clip(1.0 + 0.15 * jax.random.normal(arg_keys[3], (D,), jnp.float32), 0.25, 1.75)
    router = scatter_about(arg_keys[4], (D, EXPERTS), D ** -0.5, 0.125)
    route_ids_keys = jax.random.split(jax.random.fold_in(arg_keys[5], 1), TOKENS // TOK_DEV)
    route_ids_turns = jax.random.permutation(jax.random.fold_in(arg_keys[5], 3), TOKENS // TOK_DEV)
    route_ids = jax.vmap(lambda own, number: routed_block(jax.random.fold_in(arg_keys[5], 2), own, number, TOK_DEV, EXPERTS, TOPK, CAP, 0))(route_ids_keys, route_ids_turns).reshape((TOKENS, TOPK))
    w_gate = scatter_about(arg_keys[6], (EXPERTS, D, FF), D ** -0.5, 0.125, ((0, 64),))
    w_up = scatter_about(arg_keys[7], (EXPERTS, D, FF), D ** -0.5, 0.125, ((0, 64),))
    w_down = scatter_about(arg_keys[8], (EXPERTS, FF, D), FF ** -0.5, 0.21875, ((0, 64),))
    bias = jnp.clip(jax.random.uniform(arg_keys[9], (EXPERTS,), jnp.float32, -1.0, 1.0), -1.0, 1.0)
    gain_next = jnp.clip(1.0 + 0.15 * jax.random.normal(arg_keys[10], (D,), jnp.float32), 0.25, 1.75)
    w_query = scatter_about(arg_keys[11], (D, HEADS * HD), D ** -0.5, 0.125, ((1, 16),))
    return {"attn_heads": attn_heads, "w_out": w_out, "residual": residual, "gain_moe": gain_moe, "router": router, "route_ids": route_ids, "w_gate": w_gate, "w_up": w_up, "w_down": w_down, "bias": bias, "gain_next": gain_next, "w_query": w_query}


def rms_scale(values, gain):
    mean_sq = lax.optimization_barrier(jnp.mean(values * values, axis=-1, keepdims=True))
    return values * lax.rsqrt(mean_sq + 1e-06) * gain.astype(jnp.float32)

def reference(attn_heads, w_out, residual, gain_moe, router, route_ids, w_gate, w_up, w_down, bias, gain_next, w_query):
    attn_proj = jnp.dot(attn_heads, w_out, preferred_element_type=jnp.float32)
    stream = residual.astype(jnp.float32) + attn_proj
    normed = rms_scale(stream, gain_moe).astype(jnp.bfloat16)
    logits = jnp.dot(normed, router, preferred_element_type=jnp.float32)
    picked = jnp.take_along_axis(logits, route_ids, axis=1)
    scores = jax.nn.sigmoid(picked)
    weights = (scores / lax.optimization_barrier(jnp.sum(scores, axis=1, keepdims=True))).astype(jnp.bfloat16)
    devices = N_DP * N_FOLD * N_TENSOR
    hits = lax.optimization_barrier(jnp.sum((route_ids[:, :, None] == jnp.arange(EXPERTS, dtype=jnp.int32)[None, None, :]).astype(jnp.int32), axis=1))
    blocks = hits.reshape(devices, TOK_DEV, EXPERTS)
    before = (jnp.cumsum(blocks, axis=1) - blocks).reshape(TOKENS, EXPERTS)
    slots = jnp.take_along_axis(before, route_ids, axis=1)
    owner = jnp.arange(TOKENS, dtype=jnp.int32) // TOK_DEV
    target = owner[:, None] * CAP + slots
    empty_index = devices * CAP

    def add_expert(combined, expert):
        here = route_ids == expert
        present = jnp.any(here, axis=1)
        index = lax.optimization_barrier(jnp.sum(jnp.where(here, target, 0), axis=1)) + jnp.where(present, 0, empty_index)
        index = index.astype(jnp.int32)
        share = lax.optimization_barrier(jnp.sum(jnp.where(here, weights.astype(jnp.float32), jnp.float32(0.0)), axis=1))
        rows = jnp.zeros((empty_index, D), jnp.bfloat16).at[index].set(normed, mode='drop')
        gate = jnp.dot(rows, w_gate[expert], preferred_element_type=jnp.float32)
        upper = jnp.dot(rows, w_up[expert], preferred_element_type=jnp.float32)
        act = (jax.nn.silu(gate) * upper).astype(jnp.bfloat16)
        result = jnp.dot(act, w_down[expert], preferred_element_type=jnp.float32).astype(jnp.bfloat16)
        taken = jnp.take(result, jnp.minimum(index, empty_index - 1), axis=0).astype(jnp.float32)
        return (combined + share[:, None] * taken, None)
    combined, _ = lax.scan(add_expert, jnp.zeros((TOKENS, D), jnp.float32), jnp.arange(EXPERTS, dtype=jnp.int32))
    new_stream = stream + combined
    stream_out = new_stream.astype(jnp.bfloat16)
    normed_next = rms_scale(new_stream, gain_next).astype(jnp.bfloat16)
    query = jnp.dot(normed_next, w_query, preferred_element_type=jnp.float32).astype(jnp.bfloat16)
    counts = lax.optimization_barrier(jnp.sum(hits, axis=0))
    mean_load = TOKENS * TOPK / EXPERTS
    new_bias = bias + 0.5 * (mean_load - counts.astype(jnp.float32)) / jnp.sqrt(jnp.float32(mean_load))
    return (stream_out, query, new_bias)
```

```python
import math

import jax
import jax.numpy as jnp
from jax import lax
from jax.experimental import pallas as pl
from jax.experimental.pallas import tpu as pltpu
from jax.sharding import PartitionSpec as P

TOK = 32
HALF = 16
CAP = 6
NY = 8
NX = 4
NZ = 12
MEAN_LOAD = 3072.0

REL = (0, -1, 1, -2, 2, -3, 3, 4)
AG_SRC = ((0, 1, 3, 5), (0, 2, 4, 6))
AG_DST = ((1, 3, 5, 7), (2, 4, 6, 7))
RS_BLK = ((7, 6, 4, 2), (7, 5, 3, 1))
TILE_BLOCKS = ((0, 2), (2, 5), (5, 7))

BF = jnp.bfloat16
F32 = jnp.float32


def dot(a, b):
    return jnp.dot(a, b, preferred_element_type=F32)


def kernel(
    attn, w_out, residual, gain1, router_t, ids_t, w_gate, w_up, w_down, bias, gain2, w_query,
    stream_out, query, new_bias,
    attn_v, w_out_v, wg, wu, wd, wq,
    part, sib_send, sib_recv,
    rs1_send, rs1_recv, rs2_send, rs2_recv,
    norm, norm2, stream, comb,
    table, pick, mix,
    x_send, x_recv, y_send, y_recv,
    cx_send, cx_recv, cz_send, cz_recv,
    sem_attn, sem_w, s_sib, r_sib,
    s_rs1, r_rs1, s_rs2, r_rs2, s_ag1, r_ag1, s_ag2, r_ag2, s_agc, r_agc, s_tab, r_tab,
    s_x, r_x, s_y, r_y, s_cx, r_cx, s_cz, r_cz,
):
    z = lax.axis_index("dp")
    x = lax.axis_index("fold")
    t = lax.axis_index("tensor")
    y = t // 2
    c = t % 2
    sib = {"tensor": y * 2 + (1 - c)}
    ring = ({"tensor": (t + 2) % 16}, {"tensor": (t + 14) % 16})

    def plane(dx, cr, sign):
        core = c + cr * (1 - 2 * c)
        return {"fold": (x + sign * dx + NX) % NX, "tensor": y * 2 + core}

    pending = []

    def send(src, dst, ss, rs, dev):
        copy = pltpu.make_async_remote_copy(
            src_ref=src, dst_ref=dst, send_sem=ss, recv_sem=rs,
            device_id=dev, device_id_type=pl.DeviceIdType.MESH,
        )
        copy.start()
        pending.append(copy)
        return copy

    attn_copies = []
    for par in range(2):
        for a in range(8):
            core = c if par == 1 else 1 - c
            row = ((y + REL[a] + NY) % NY * 2 + core) * TOK
            copy = pltpu.make_async_copy(
                attn.at[pl.ds(pl.multiple_of(row, TOK), TOK), :],
                attn_v.at[pl.ds((par * 8 + a) * TOK, TOK), :],
                sem_attn.at[par * 8 + a],
            )
            copy.start()
            attn_copies.append(copy)
    w_copies = []
    for i, (src, dst) in enumerate(
        ((w_out, w_out_v), (w_gate.at[0], wg), (w_up.at[0], wu), (w_down.at[0], wd), (w_query, wq))
    ):
        copy = pltpu.make_async_copy(src, dst, sem_w.at[i])
        copy.start()
        w_copies.append(copy)

    barrier = pltpu.get_barrier_semaphore()
    peers = [ring[0], ring[1], sib]
    for dx in range(1, NX):
        for cr in range(2):
            peers.append(plane(dx, cr, 1))
    for dz in range(1, NZ):
        peers.append({"dp": (z + dz) % NZ})
    for peer in peers:
        pl.semaphore_signal(barrier, inc=1, device_id=peer, device_id_type=pl.DeviceIdType.MESH)
    pl.semaphore_wait(barrier, len(peers))

    expert = lax.broadcasted_iota(jnp.int32, (128, TOK), 0)
    hit = jnp.zeros((128, TOK), F32)
    for k in range(8):
        hit = hit + jnp.where(expert == ids_t[k : k + 1, :], 1.0, 0.0)
    rows = lax.broadcasted_iota(jnp.int32, (TOK, TOK), 0)
    cols = lax.broadcasted_iota(jnp.int32, (TOK, TOK), 1)
    before = dot(hit.astype(BF), jnp.where(rows < cols, 1.0, 0.0).astype(BF))
    slot = jnp.where(hit > 0.5, before, -1.0).astype(BF)
    eye = jnp.where(rows == cols, 1.0, 0.0).astype(BF)
    own_table = lax.dot_general(eye, slot, (((1,), (1,)), ((), ())), preferred_element_type=F32)
    table[0:TOK, :] = own_table.astype(BF)

    def table_send(d, s):
        return send(
            table.at[pl.ds(AG_SRC[d][s] * TOK, TOK), :],
            table.at[pl.ds(AG_DST[d][s] * TOK, TOK), :],
            s_tab.at[d * 4 + s], r_tab.at[d * 4 + s], ring[d],
        )

    tab = {}
    for d in range(2):
        tab[d, 0] = table_send(d, 0)

    w_copies[0].wait()
    for a in range(8):
        attn_copies[a].wait()
    sib_copies = []
    for piece in (1, 0):
        lo = piece * 128
        for col in range(0, 2048, 512):
            sib_send[lo : lo + 128, col : col + 512] = dot(
                attn_v[lo : lo + 128, :], w_out_v[:, col : col + 512]
            ).astype(BF)
        sib_copies.append(
            send(
                sib_send.at[pl.ds(lo, 128), :], sib_recv.at[pl.ds(lo, 128), :],
                s_sib.at[piece], r_sib.at[piece], sib,
            )
        )
    for a in range(8):
        attn_copies[8 + a].wait()
    for col in range(0, 2048, 512):
        part[:, col : col + 512] = dot(attn_v[256:512, :], w_out_v[:, col : col + 512])

    def rs_step(s, own, send_buf, recv_buf, ss, rs, copies):
        for h in range(2):
            for d in range(2):
                if s == 0 and h != d:
                    continue
                idx = d * 8 + s * 2 + h
                value = own(RS_BLK[d][s], h)
                if (d, s - 1, h) in copies:
                    copies[d, s - 1, h].wait_recv()
                    prev = (idx - 2) * HALF
                    value = value + recv_buf[prev : prev + HALF, :].astype(F32)
                here = pl.ds(idx * HALF, HALF)
                send_buf[idx * HALF : (idx + 1) * HALF, :] = value.astype(BF)
                copies[d, s, h] = send(
                    send_buf.at[here, :], recv_buf.at[here, :], ss.at[idx], rs.at[idx], ring[d]
                )

    def rs_last(h, own, recv_buf, copies):
        value = own(0, h)
        for d in range(2):
            copies[d, 3, h].wait_recv()
            at = (d * 8 + 6 + h) * HALF
            value = value + recv_buf[at : at + HALF, :].astype(F32)
        return value

    def own1(a, h):
        at = a * TOK + h * HALF
        return part[at : at + HALF, :] + sib_recv[at : at + HALF, :].astype(F32)

    rs1 = {}
    sib_copies[0].wait_recv()
    for s in range(2):
        rs_step(s, own1, rs1_send, rs1_recv, s_rs1, r_rs1, rs1)
        for d in range(2):
            tab[d, s].wait_recv()
            tab[d, s + 1] = table_send(d, s + 1)
    sib_copies[1].wait_recv()
    rs_step(2, own1, rs1_send, rs1_recv, s_rs1, r_rs1, rs1)
    for d in range(2):
        tab[d, 2].wait_recv()
    tab[0, 3] = table_send(0, 3)
    rs_step(3, own1, rs1_send, rs1_recv, s_rs1, r_rs1, rs1)
    tab[0, 3].wait_recv()

    all_slots = table[...].astype(F32)
    count = jnp.sum(jnp.where(all_slots > -0.5, 1.0, 0.0), axis=0, keepdims=True)
    cx_send[...] = jnp.broadcast_to(count, (8, 128))
    cx = []
    for dest in range(1, 8):
        cx.append(
            send(
                cx_send, cx_recv.at[pl.ds(dest * 8, 8), :],
                s_cx.at[dest], r_cx.at[dest], plane(dest // 2, dest % 2, 1),
            )
        )

    e_at = lax.broadcasted_iota(jnp.int32, (128, 384), 0)
    r_at = lax.broadcasted_iota(jnp.int32, (128, 384), 1)
    dest_at = (r_at >> 4) & 7
    cr_at = dest_at & 1
    e_of = ((x + (dest_at >> 1)) & 3) * 16 + y * 2 + c + cr_at * (1 - 2 * c)
    select = jnp.where(e_at == e_of, 1.0, 0.0).astype(BF)
    r_row = lax.broadcasted_iota(jnp.int32, (256, 384), 1)
    packed = (r_row >> 7) * 16 + (r_row & 15)
    block_of = (packed * 43) >> 8
    slot_of = (packed - block_of * 6).astype(F32)
    tok_block = lax.broadcasted_iota(jnp.int32, (256, 384), 0) >> 5
    spread = dot(table[...], select)
    match = jnp.logical_and(spread == slot_of, tok_block == block_of)
    pick[...] = jnp.where(match, 1.0, 0.0)

    def normalize(value, gain):
        mean_sq = jnp.mean(value * value, axis=-1, keepdims=True)
        return (value * lax.rsqrt(mean_sq + 1e-06) * gain[...]).astype(BF)

    def ag_send(buf, scale, d, s, h, ss, rs):
        src = AG_SRC[d][s] * scale + h * HALF
        dst = AG_DST[d][s] * scale + h * HALF
        idx = d * 8 + s * 2 + h
        return send(
            buf.at[pl.ds(src, HALF), :], buf.at[pl.ds(dst, HALF), :], ss.at[idx], rs.at[idx], ring[d]
        )

    ag1 = {}
    for h in range(2):
        at = h * HALF
        value = residual[at : at + HALF, :].astype(F32) + rs_last(h, own1, rs1_recv, rs1)
        stream[at : at + HALF, :] = value
        norm[at : at + HALF, :] = normalize(value, gain1)
        for d in range(2):
            ag1[d, 0, h] = ag_send(norm, TOK, d, 0, h, s_ag1, r_ag1)

    def ag1_pass(s):
        for h in range(2):
            for d in range(2):
                if (d, s, h) not in ag1:
                    continue
                ag1[d, s, h].wait_recv()
                if s < 2 or (s == 2 and h == d):
                    ag1[d, s + 1, h] = ag_send(norm, TOK, d, s + 1, h, s_ag1, r_ag1)

    xs = {}

    def dispatch(g):
        lo, hi = TILE_BLOCKS[g][0] * TOK, (TILE_BLOCKS[g][1] + 1) * TOK
        lhs = pick[lo:hi, g * 128 : (g + 1) * 128].T.astype(BF)
        for col in range(0, 2048, 512):
            x_send[g * 128 : (g + 1) * 128, col : col + 512] = dot(
                lhs, norm[lo:hi, col : col + 512]
            ).astype(BF)
        for dest in (4, 5, 2, 3, 6, 7, 1):
            at = pl.ds(g * 128 + dest * HALF, HALF)
            xs[g, dest] = send(
                x_send.at[at, :], x_recv.at[at, :],
                s_x.at[g * 8 + dest], r_x.at[g * 8 + dest], plane(dest // 2, dest % 2, 1),
            )
        x_recv[g * 128 : g * 128 + HALF, :] = x_send[g * 128 : g * 128 + HALF, :]

    ag1_pass(0)
    dispatch(0)
    ag1_pass(1)
    ag1_pass(2)
    dispatch(1)
    ag1_pass(3)
    dispatch(2)

    logits = lax.dot_general(
        norm[...], router_t[...], (((1,), (1,)), ((), ())), preferred_element_type=F32
    )
    score = 1.0 / (1.0 + jnp.exp(-logits))
    score = jnp.where(table[:, 0:64].astype(F32) > -0.5, score, 0.0)
    weight = (score / jnp.sum(score, axis=1, keepdims=True)).astype(BF)
    mix[...] = (dot(weight, select[0:64, :]) * pick[...]).astype(BF)

    total = cx_send[...]
    for dest in range(1, 8):
        cx[dest - 1].wait_recv()
        total = total + cx_recv[dest * 8 : dest * 8 + 8, :]
    cz_send[...] = total
    cz = []
    for dz in range(1, NZ):
        cz.append(
            send(
                cz_send, cz_recv.at[pl.ds(dz * 8, 8), :],
                s_cz.at[dz], r_cz.at[dz], {"dp": (z + dz) % NZ},
            )
        )

    w_copies[1].wait()
    w_copies[2].wait()
    w_copies[3].wait()
    for g in range(3):
        for dest in (2, 3, 6, 7, 4, 5, 1):
            xs[g, dest].wait_recv()
        arrived = x_recv[g * 128 : (g + 1) * 128, :]
        gate = dot(arrived, wg[...])
        upper = dot(arrived, wu[...])
        act = (gate / (1.0 + jnp.exp(-gate)) * upper).astype(BF)
        for col in range(0, 2048, 512):
            y_send[g * 128 : (g + 1) * 128, col : col + 512] = dot(
                act, wd[:, col : col + 512]
            ).astype(BF)

    ys = {}
    for g in (2, 1, 0):
        for dest in (4, 5, 2, 3, 6, 7, 1):
            at = pl.ds(g * 128 + dest * HALF, HALF)
            ys[g, dest] = send(
                y_send.at[at, :], y_recv.at[at, :],
                s_y.at[g * 8 + dest], r_y.at[g * 8 + dest], plane(dest // 2, dest % 2, -1),
            )
        y_recv[g * 128 : g * 128 + HALF, :] = y_send[g * 128 : g * 128 + HALF, :]

    def own2(a, h):
        at = a * TOK + h * HALF
        return comb[at : at + HALF, :]

    def mixdown(g):
        for dest in (2, 3, 6, 7, 4, 5, 1):
            ys[g, dest].wait_recv()
        lo, hi = TILE_BLOCKS[g][0] * TOK, (TILE_BLOCKS[g][1] + 1) * TOK
        for col in range(0, 2048, 512):
            value = dot(
                mix[lo:hi, g * 128 : (g + 1) * 128],
                y_recv[g * 128 : (g + 1) * 128, col : col + 512],
            )
            if g == 2:
                comb[lo:hi, col : col + 512] = value
            else:
                comb[lo : hi - TOK, col : col + 512] = value[: hi - TOK - lo, :]
                comb[hi - TOK : hi, col : col + 512] += value[hi - TOK - lo :, :]

    rs2 = {}
    mixdown(2)
    rs_step(0, own2, rs2_send, rs2_recv, s_rs2, r_rs2, rs2)
    mixdown(1)
    rs_step(1, own2, rs2_send, rs2_recv, s_rs2, r_rs2, rs2)
    rs_step(2, own2, rs2_send, rs2_recv, s_rs2, r_rs2, rs2)
    mixdown(0)
    rs_step(3, own2, rs2_send, rs2_recv, s_rs2, r_rs2, rs2)

    total = cz_send[...]
    for dz in range(1, NZ):
        cz[dz - 1].wait_recv()
        total = total + cz_recv[dz * 8 : dz * 8 + 8, :]
    new_bias[...] = bias[...] + 0.5 * (MEAN_LOAD - total[0:1, 0:64]) / math.sqrt(MEAN_LOAD)

    ag2 = {}
    agc = {}

    def share(a, h):
        src = pl.ds(a * 2 * TOK + h * HALF, HALF)
        dst = pl.ds((a * 2 + 1) * TOK + h * HALF, HALF)
        agc[a, h] = send(
            norm2.at[src, :], norm2.at[dst, :], s_agc.at[a * 2 + h], r_agc.at[a * 2 + h], sib
        )

    for h in range(2):
        at = h * HALF
        value = stream[at : at + HALF, :] + rs_last(h, own2, rs2_recv, rs2)
        stream_out[at : at + HALF, :] = value.astype(BF)
        norm2[at : at + HALF, :] = normalize(value, gain2)
        for d in range(2):
            ag2[d, 0, h] = ag_send(norm2, 2 * TOK, d, 0, h, s_ag2, r_ag2)
        share(0, h)

    def ag2_pass(s):
        for h in range(2):
            for d in range(2):
                if (d, s, h) not in ag2:
                    continue
                ag2[d, s, h].wait_recv()
                if s < 2 or (s == 2 and h == d):
                    ag2[d, s + 1, h] = ag_send(norm2, 2 * TOK, d, s + 1, h, s_ag2, r_ag2)
                share(AG_DST[d][s], h)

    def project(first, last):
        for a in range(first, last + 1):
            for h in range(2):
                agc[a, h].wait_recv()
        lo, hi = first * 2 * TOK, (last + 1) * 2 * TOK
        value = dot(norm2[lo:hi, :], wq[...]).astype(BF)
        for a in range(first, last + 1):
            for par in range(2):
                core = c if par == 0 else 1 - c
                row = ((y + REL[a] + NY) % NY * 2 + core) * TOK
                at = ((a - first) * 2 + par) * TOK
                query[pl.ds(pl.multiple_of(row, TOK), TOK), :] = value[at : at + TOK, :]

    w_copies[4].wait()
    ag2_pass(0)
    project(0, 0)
    ag2_pass(1)
    project(1, 2)
    ag2_pass(2)
    project(3, 4)
    ag2_pass(3)
    project(5, 6)
    project(7, 7)

    for copy in pending:
        copy.wait_send()


def local(
    attn_heads, w_out, residual, gain_moe, router, route_ids,
    w_gate, w_up, w_down, bias, gain_next, w_query,
):
    width = residual.shape[1]
    vmem = pl.BlockSpec(memory_space=pltpu.VMEM)
    hbm = pl.BlockSpec(memory_space=pl.ANY)
    dma = pltpu.SemaphoreType.DMA
    scratch = [
        pltpu.VMEM((512, 256), BF), pltpu.VMEM((256, 2048), BF),
        pltpu.VMEM((2048, 768), BF), pltpu.VMEM((2048, 768), BF),
        pltpu.VMEM((768, 2048), BF), pltpu.VMEM((2048, 256), BF),
        pltpu.VMEM((256, width), F32), pltpu.VMEM((256, width), BF), pltpu.VMEM((256, width), BF),
        pltpu.VMEM((256, width), BF), pltpu.VMEM((256, width), BF),
        pltpu.VMEM((256, width), BF), pltpu.VMEM((256, width), BF),
        pltpu.VMEM((256, width), BF), pltpu.VMEM((512, width), BF),
        pltpu.VMEM((TOK, width), F32), pltpu.VMEM((256, width), F32),
        pltpu.VMEM((256, 128), BF), pltpu.VMEM((256, 384), F32), pltpu.VMEM((256, 384), BF),
        pltpu.VMEM((384, width), BF), pltpu.VMEM((384, width), BF),
        pltpu.VMEM((384, width), BF), pltpu.VMEM((384, width), BF),
        pltpu.VMEM((8, 128), F32), pltpu.VMEM((64, 128), F32),
        pltpu.VMEM((8, 128), F32), pltpu.VMEM((96, 128), F32),
        dma((16,)), dma((5,)), dma((2,)), dma((2,)),
        dma((16,)), dma((16,)), dma((16,)), dma((16,)),
        dma((16,)), dma((16,)), dma((16,)), dma((16,)),
        dma((16,)), dma((16,)), dma((8,)), dma((8,)),
        dma((24,)), dma((24,)), dma((24,)), dma((24,)),
        dma((8,)), dma((8,)), dma((12,)), dma((12,)),
    ]
    stream_out, query, new_bias = pl.pallas_call(
        kernel,
        out_shape=(
            jax.ShapeDtypeStruct((TOK, width), BF),
            jax.ShapeDtypeStruct((512, 256), BF),
            jax.ShapeDtypeStruct((1, 64), F32),
        ),
        in_specs=[hbm, hbm, vmem, vmem, vmem, vmem, hbm, hbm, hbm, vmem, vmem, hbm],
        out_specs=(vmem, vmem, vmem),
        scratch_shapes=scratch,
        compiler_params=pltpu.CompilerParams(
            collective_id=0, has_side_effects=True, vmem_limit_bytes=52 * 1024 * 1024
        ),
    )(
        attn_heads, w_out, residual, gain_moe.reshape(1, -1), router.T, route_ids.T,
        w_gate, w_up, w_down, bias.reshape(1, -1), gain_next.reshape(1, -1), w_query,
    )
    return stream_out, query, new_bias.reshape(-1)


def solution(mesh):
    in_specs = (
        P(("dp", "fold"), "tensor"),
        P("tensor", None),
        P(("dp", "fold", "tensor"), None),
        P(),
        P(),
        P(("dp", "fold", "tensor"), None),
        P(("fold", "tensor"), None, None),
        P(("fold", "tensor"), None, None),
        P(("fold", "tensor"), None, None),
        P(),
        P(),
        P(None, "tensor"),
    )
    out_specs = (P(("dp", "fold", "tensor"), None), P(("dp", "fold"), "tensor"), P())
    return jax.shard_map(local, mesh=mesh, in_specs=in_specs, out_specs=out_specs, check_vma=False)
```

```python
import math

import jax
import jax.numpy as jnp
from jax import lax
from jax.experimental import pallas as pl
from jax.experimental.pallas import tpu as pltpu
from jax.sharding import PartitionSpec as P

TOK = 32
HALF = 16
CAP = 6
NY = 8
NX = 4
NZ = 12
MEAN_LOAD = 3072.0

REL = (0, -1, 1, -2, 2, -3, 3, 4)
AG_SRC = ((0, 1, 3, 5), (0, 2, 4, 6))
AG_DST = ((1, 3, 5, 7), (2, 4, 6, 7))
RS_BLK = ((7, 6, 4, 2), (7, 5, 3, 1))
TILE_BLOCKS = ((0, 2), (2, 5), (5, 7))

BF = jnp.bfloat16
F32 = jnp.float32


def dot(a, b):
    return jnp.dot(a, b, preferred_element_type=F32)


def kernel(
    attn, w_out, residual_h, gain1_h, router_h, ids_h, w_gate, w_up, w_down, bias_h, gain2_h, w_query,
    stream_out, query, new_bias,
    attn_v, attn_o, w_out_v, wg, wu, wd, wq,
    residual, gain1, router_t, ids_t, bias, gain2,
    part, sib_send, sib_recv,
    rs1_send, rs1_recv, rs2_send, rs2_recv,
    norm, norm2, stream, comb,
    table, pick, pick_t, mix,
    x_send, x_recv, y_send, y_recv,
    cx_send, cx_recv, cz,
    sem_load, s_sib, r_sib,
    s_rs1, r_rs1, s_rs2, r_rs2, s_ag1, r_ag1, s_ag2, r_ag2, s_agc, r_agc, s_tab, r_tab,
    s_x, r_x, s_y, r_y, s_cx, r_cx, s_cz, r_cz,
):
    z = lax.axis_index("dp")
    x = lax.axis_index("fold")
    t = lax.axis_index("tensor")
    y = t // 2
    c = t % 2
    sib = {"tensor": y * 2 + (1 - c)}
    ring = ({"tensor": (t + 2) % 16}, {"tensor": (t + 14) % 16})

    def plane(dx, cr, sign):
        core = c + cr * (1 - 2 * c)
        return {"fold": (x + sign * dx + NX) % NX, "tensor": y * 2 + core}

    pending = []

    def send(src, dst, ss, rs, dev):
        copy = pltpu.make_async_remote_copy(
            src_ref=src, dst_ref=dst, send_sem=ss, recv_sem=rs,
            device_id=dev, device_id_type=pl.DeviceIdType.MESH,
        )
        copy.start()
        pending.append(copy)
        return copy

    barrier = pltpu.get_barrier_semaphore()
    peers = [sib, ring[0], ring[1]]
    for dx in range(1, NX):
        for cr in range(2):
            peers.append(plane(dx, cr, 1))
    for peer in peers:
        pl.semaphore_signal(barrier, inc=1, device_id=peer, device_id_type=pl.DeviceIdType.MESH)
    for k in range(1, NZ):

        @pl.when(z + k < NZ)
        def _(k=k):
            pl.semaphore_signal(
                barrier, inc=1, device_id={"dp": (z + k) % NZ}, device_id_type=pl.DeviceIdType.MESH
            )

    def load(i, src, dst):
        copy = pltpu.make_async_copy(src, dst, sem_load.at[i])
        copy.start()
        return copy

    load_ids = load(0, ids_h, ids_t)
    load_attn = load(1, attn, attn_v)
    load_w_out = load(2, w_out, w_out_v)
    load_residual = load(3, residual_h, residual)
    load_gain1 = load(4, gain1_h, gain1)
    load_router = load(5, router_h, router_t)

    load_ids.wait()
    expert = lax.broadcasted_iota(jnp.int32, (128, TOK), 0)
    hit = jnp.zeros((128, TOK), F32)
    for k in range(8):
        hit = hit + jnp.where(expert == ids_t[k : k + 1, :], 1.0, 0.0)
    rows = lax.broadcasted_iota(jnp.int32, (TOK, TOK), 0)
    cols = lax.broadcasted_iota(jnp.int32, (TOK, TOK), 1)
    before = dot(hit.astype(BF), jnp.where(rows < cols, 1.0, 0.0).astype(BF))
    slot = jnp.where(hit > 0.5, before, -1.0).astype(BF)
    eye = jnp.where(rows == cols, 1.0, 0.0).astype(BF)
    own_table = lax.dot_general(eye, slot, (((1,), (1,)), ((), ())), preferred_element_type=F32)
    table[0:TOK, :] = own_table.astype(BF)

    def table_send(d, s):
        return send(
            table.at[pl.ds(AG_SRC[d][s] * TOK, TOK), :],
            table.at[pl.ds(AG_DST[d][s] * TOK, TOK), :],
            s_tab.at[d * 4 + s], r_tab.at[d * 4 + s], ring[d],
        )

    load_attn.wait()
    for par in range(2):
        for a in range(8):
            core = c if par == 1 else 1 - c
            row = ((y + REL[a] + NY) % NY * 2 + core) * TOK
            at = (par * 8 + a) * TOK
            attn_o[at : at + TOK, :] = attn_v[pl.ds(pl.multiple_of(row, TOK), TOK), :]
    load_w_out.wait()
    tab = {}
    sib_copies = {}
    for lo in (128, 0):
        for col in range(0, 2048, 512):
            sib_send[lo : lo + 128, col : col + 512] = dot(
                attn_o[lo : lo + 128, :], w_out_v[:, col : col + 512]
            ).astype(BF)
        if lo == 128:
            pl.semaphore_wait(barrier, len(peers) + z)
            for d in range(2):
                tab[d, 0] = table_send(d, 0)
        for a in range(lo // TOK + 3, lo // TOK - 1, -1):
            here = pl.ds(a * TOK, TOK)
            sib_copies[a] = send(
                sib_send.at[here, :], sib_recv.at[here, :], s_sib.at[a], r_sib.at[a], sib
            )
    for lo in (384, 256):
        for col in range(0, 2048, 512):
            part[lo - 256 : lo - 128, col : col + 512] = dot(
                attn_o[lo : lo + 128, :], w_out_v[:, col : col + 512]
            )
    load_wg = load(6, w_gate.at[0], wg)
    load_wu = load(7, w_up.at[0], wu)
    load_wd = load(8, w_down.at[0], wd)
    load_wq = load(9, w_query, wq)
    load_bias = load(10, bias_h, bias)
    load_gain2 = load(11, gain2_h, gain2)

    def rs_step(s, own, send_buf, recv_buf, ss, rs, copies):
        order = ((0, 0), (1, 1)) if s == 0 else ((0, 1), (1, 0), (0, 0), (1, 1))
        for d, h in order:
            idx = d * 8 + s * 2 + h
            value = own(RS_BLK[d][s], h)
            if (d, s - 1, h) in copies:
                copies[d, s - 1, h].wait_recv()
                prev = (idx - 2) * HALF
                value = value + recv_buf[prev : prev + HALF, :].astype(F32)
            here = pl.ds(idx * HALF, HALF)
            send_buf[idx * HALF : (idx + 1) * HALF, :] = value.astype(BF)
            copies[d, s, h] = send(
                send_buf.at[here, :], recv_buf.at[here, :], ss.at[idx], rs.at[idx], ring[d]
            )

    def rs_last(h, own, recv_buf, copies):
        value = own(0, h)
        for d in range(2):
            copies[d, 3, h].wait_recv()
            at = (d * 8 + 6 + h) * HALF
            value = value + recv_buf[at : at + HALF, :].astype(F32)
        return value

    def own1(a, h):
        at = a * TOK + h * HALF
        return part[at : at + HALF, :] + sib_recv[at : at + HALF, :].astype(F32)

    sib_here = set()

    def sib_wait(*blocks):
        for a in blocks:
            if a not in sib_here:
                sib_here.add(a)
                sib_copies[a].wait_recv()

    rs1 = {}
    for s in range(3):
        sib_wait(RS_BLK[0][s], RS_BLK[1][s])
        rs_step(s, own1, rs1_send, rs1_recv, s_rs1, r_rs1, rs1)
        for d in range(2):
            tab[d, s].wait_recv()
            if s < 2 or d == 0:
                tab[d, s + 1] = table_send(d, s + 1)
    sib_wait(2, 1, 0)
    rs_step(3, own1, rs1_send, rs1_recv, s_rs1, r_rs1, rs1)
    tab[0, 3].wait_recv()

    all_slots = table[...].astype(F32)
    count = jnp.sum(jnp.where(all_slots > -0.5, 1.0, 0.0), axis=0, keepdims=True)
    cx_send[...] = jnp.broadcast_to(count, (8, 128))
    cx = []
    for dest in range(1, 8):
        cx.append(
            send(
                cx_send, cx_recv.at[pl.ds(dest * 8, 8), :],
                s_cx.at[dest], r_cx.at[dest], plane(dest // 2, dest % 2, 1),
            )
        )

    e_at = lax.broadcasted_iota(jnp.int32, (128, 384), 0)
    r_at = lax.broadcasted_iota(jnp.int32, (128, 384), 1)
    dest_at = (r_at >> 4) & 7
    cr_at = dest_at & 1
    e_of = ((x + (dest_at >> 1)) & 3) * 16 + y * 2 + c + cr_at * (1 - 2 * c)
    select = jnp.where(e_at == e_of, 1.0, 0.0).astype(BF)
    r_row = lax.broadcasted_iota(jnp.int32, (256, 384), 1)
    packed = (r_row >> 7) * 16 + (r_row & 15)
    block_of = (packed * 43) >> 8
    slot_of = (packed - block_of * 6).astype(F32)
    tok_block = lax.broadcasted_iota(jnp.int32, (256, 384), 0) >> 5
    spread = dot(table[...], select)
    match = jnp.logical_and(spread == slot_of, tok_block == block_of)
    pick[...] = jnp.where(match, 1.0, 0.0)
    pick_t[...] = pick[...].T.astype(BF)
    load_residual.wait()
    load_gain1.wait()

    def normalize(value, gain):
        mean_sq = jnp.mean(value * value, axis=-1, keepdims=True)
        return (value * lax.rsqrt(mean_sq + 1e-06) * gain[...]).astype(BF)

    def ag_send(buf, scale, d, s, h, ss, rs):
        src = AG_SRC[d][s] * scale + h * HALF
        dst = AG_DST[d][s] * scale + h * HALF
        idx = d * 8 + s * 2 + h
        return send(
            buf.at[pl.ds(src, HALF), :], buf.at[pl.ds(dst, HALF), :], ss.at[idx], rs.at[idx], ring[d]
        )

    ag1 = {}
    for h in range(2):
        at = h * HALF
        value = residual[at : at + HALF, :].astype(F32) + rs_last(h, own1, rs1_recv, rs1)
        stream[at : at + HALF, :] = value
        norm[at : at + HALF, :] = normalize(value, gain1)
        for d in range(2):
            ag1[d, 0, h] = ag_send(norm, TOK, d, 0, h, s_ag1, r_ag1)

    def ag1_pass(s):
        for h in range(2):
            for d in range(2):
                if (d, s, h) not in ag1:
                    continue
                ag1[d, s, h].wait_recv()
                if s < 2 or (s == 2 and h == d):
                    ag1[d, s + 1, h] = ag_send(norm, TOK, d, s + 1, h, s_ag1, r_ag1)

    xs = {}

    def dispatch(g):
        lo, hi = TILE_BLOCKS[g][0] * TOK, (TILE_BLOCKS[g][1] + 1) * TOK
        lhs = pick_t[g * 128 : (g + 1) * 128, lo:hi]
        for col in range(0, 2048, 512):
            x_send[g * 128 : (g + 1) * 128, col : col + 512] = dot(
                lhs, norm[lo:hi, col : col + 512]
            ).astype(BF)
        for dest in (4, 5, 2, 3, 6, 7, 1):
            at = pl.ds(g * 128 + dest * HALF, HALF)
            xs[g, dest] = send(
                x_send.at[at, :], x_recv.at[at, :],
                s_x.at[g * 8 + dest], r_x.at[g * 8 + dest], plane(dest // 2, dest % 2, 1),
            )
        x_recv[g * 128 : g * 128 + HALF, :] = x_send[g * 128 : g * 128 + HALF, :]

    def z_copy(k):
        return pltpu.make_async_remote_copy(
            src_ref=cz.at[pl.ds(0, 8), :], dst_ref=cz.at[pl.ds(k * 8, 8), :],
            send_sem=s_cz.at[k], recv_sem=r_cz.at[k],
            device_id={"dp": (z + NZ - k) % NZ}, device_id_type=pl.DeviceIdType.MESH,
        )

    def z_each(cond, act):
        for k in range(1, NZ):

            @pl.when(cond(k))
            def _(k=k):
                act(z_copy(k))

    ag1_pass(0)
    dispatch(0)
    ag1_pass(1)
    ag1_pass(2)
    dispatch(1)
    total = cx_send[...]
    for dest in range(1, 8):
        cx[dest - 1].wait_recv()
        total = total + cx_recv[dest * 8 : dest * 8 + 8, :]
    cz[0:8, :] = total
    z_each(lambda k: k <= z, lambda copy: copy.start())
    ag1_pass(3)
    dispatch(2)
    load_router.wait()

    logits = lax.dot_general(
        norm[...], router_t[...], (((1,), (1,)), ((), ())), preferred_element_type=F32
    )
    score = 1.0 / (1.0 + jnp.exp(-logits))
    score = jnp.where(table[:, 0:64].astype(F32) > -0.5, score, 0.0)
    weight = (score / jnp.sum(score, axis=1, keepdims=True)).astype(BF)
    mix[...] = (dot(weight, select[0:64, :]) * pick[...]).astype(BF)

    load_wg.wait()
    load_wu.wait()
    load_wd.wait()
    ys = {}

    def give_back(g, dests):
        for dest in dests:
            at = pl.ds(g * 128 + dest * HALF, HALF)
            ys[g, dest] = send(
                y_send.at[at, :], y_recv.at[at, :],
                s_y.at[g * 8 + dest], r_y.at[g * 8 + dest], plane(dest // 2, dest % 2, -1),
            )

    for g in range(3):
        for dest in (2, 3, 6, 7, 4, 5, 1):
            xs[g, dest].wait_recv()
        if g == 2:
            give_back(0, (2, 3, 6, 7))
        arrived = x_recv[g * 128 : (g + 1) * 128, :]
        gate = dot(arrived, wg[...])
        upper = dot(arrived, wu[...])
        act = (gate / (1.0 + jnp.exp(-gate)) * upper).astype(BF)
        for col in range(0, 2048, 512):
            y_send[g * 128 : (g + 1) * 128, col : col + 512] = dot(
                act, wd[:, col : col + 512]
            ).astype(BF)
        if g == 2:
            z_each(lambda k: z + k < NZ, lambda copy: copy.wait_recv())
            z_each(lambda k: k > z, lambda copy: copy.start())

    give_back(2, (4, 5, 2, 3, 6, 7, 1))
    give_back(1, (4, 5, 2, 3, 6, 7, 1))
    give_back(0, (4, 5, 1))
    for g in range(3):
        y_recv[g * 128 : g * 128 + HALF, :] = y_send[g * 128 : g * 128 + HALF, :]

    def own2(a, h):
        at = a * TOK + h * HALF
        return comb[at : at + HALF, :]

    def mixdown(g):
        for dest in (2, 3, 6, 7, 4, 5, 1):
            ys[g, dest].wait_recv()
        lo, hi = TILE_BLOCKS[g][0] * TOK, (TILE_BLOCKS[g][1] + 1) * TOK
        for col in range(0, 2048, 512):
            value = dot(
                mix[lo:hi, g * 128 : (g + 1) * 128],
                y_recv[g * 128 : (g + 1) * 128, col : col + 512],
            )
            if g == 2:
                comb[lo:hi, col : col + 512] = value
            else:
                comb[lo : hi - TOK, col : col + 512] = value[: hi - TOK - lo, :]
                comb[hi - TOK : hi, col : col + 512] += value[hi - TOK - lo :, :]

    rs2 = {}
    mixdown(2)
    rs_step(0, own2, rs2_send, rs2_recv, s_rs2, r_rs2, rs2)
    mixdown(1)
    rs_step(1, own2, rs2_send, rs2_recv, s_rs2, r_rs2, rs2)
    rs_step(2, own2, rs2_send, rs2_recv, s_rs2, r_rs2, rs2)
    mixdown(0)
    rs_step(3, own2, rs2_send, rs2_recv, s_rs2, r_rs2, rs2)

    z_each(lambda k: z + k >= NZ, lambda copy: copy.wait_recv())
    total = cz[0:1, :]
    for dz in range(1, NZ):
        total = total + cz[dz * 8 : dz * 8 + 1, :]
    load_bias.wait()
    new_bias[...] = bias[...] + 0.5 * (MEAN_LOAD - total[:, 0:64]) / math.sqrt(MEAN_LOAD)
    load_gain2.wait()

    ag2 = {}
    agc = {}

    def share(a, h):
        src = pl.ds(a * 2 * TOK + h * HALF, HALF)
        dst = pl.ds((a * 2 + 1) * TOK + h * HALF, HALF)
        agc[a, h] = send(
            norm2.at[src, :], norm2.at[dst, :], s_agc.at[a * 2 + h], r_agc.at[a * 2 + h], sib
        )

    for h in range(2):
        at = h * HALF
        value = stream[at : at + HALF, :] + rs_last(h, own2, rs2_recv, rs2)
        stream_out[at : at + HALF, :] = value.astype(BF)
        norm2[at : at + HALF, :] = normalize(value, gain2)
        for d in range(2):
            ag2[d, 0, h] = ag_send(norm2, 2 * TOK, d, 0, h, s_ag2, r_ag2)
        share(0, h)

    def ag2_pass(s):
        for h in range(2):
            for d in range(2):
                if (d, s, h) not in ag2:
                    continue
                ag2[d, s, h].wait_recv()
                if s < 2 or (s == 2 and h == d):
                    ag2[d, s + 1, h] = ag_send(norm2, 2 * TOK, d, s + 1, h, s_ag2, r_ag2)
                share(AG_DST[d][s], h)

    def project(first, last):
        for a in range(first, last + 1):
            for h in range(2):
                agc[a, h].wait_recv()
        lo, hi = first * 2 * TOK, (last + 1) * 2 * TOK
        value = dot(norm2[lo:hi, :], wq[...]).astype(BF)
        for a in range(first, last + 1):
            for par in range(2):
                core = c if par == 0 else 1 - c
                row = ((y + REL[a] + NY) % NY * 2 + core) * TOK
                at = ((a - first) * 2 + par) * TOK
                query[pl.ds(pl.multiple_of(row, TOK), TOK), :] = value[at : at + TOK, :]

    load_wq.wait()
    ag2_pass(0)
    project(0, 0)
    ag2_pass(1)
    project(1, 2)
    ag2_pass(2)
    project(3, 4)
    ag2_pass(3)
    project(5, 6)
    project(7, 7)

    for copy in pending:
        copy.wait_send()
    for k in range(1, NZ):
        z_copy(k).wait_send()


def local(
    attn_heads, w_out, residual, gain_moe, router, route_ids,
    w_gate, w_up, w_down, bias, gain_next, w_query,
):
    width = residual.shape[1]
    vmem = pl.BlockSpec(memory_space=pltpu.VMEM)
    hbm = pl.BlockSpec(memory_space=pl.ANY)
    dma = pltpu.SemaphoreType.DMA
    scratch = [
        pltpu.VMEM((512, 256), BF), pltpu.VMEM((512, 256), BF), pltpu.VMEM((256, 2048), BF),
        pltpu.VMEM((2048, 768), BF), pltpu.VMEM((2048, 768), BF),
        pltpu.VMEM((768, 2048), BF), pltpu.VMEM((2048, 256), BF),
        pltpu.VMEM((TOK, width), BF), pltpu.VMEM((1, width), F32), pltpu.VMEM((64, width), BF),
        pltpu.VMEM((8, TOK), jnp.int32), pltpu.VMEM((1, 64), F32), pltpu.VMEM((1, width), F32),
        pltpu.VMEM((256, width), F32), pltpu.VMEM((256, width), BF), pltpu.VMEM((256, width), BF),
        pltpu.VMEM((256, width), BF), pltpu.VMEM((256, width), BF),
        pltpu.VMEM((256, width), BF), pltpu.VMEM((256, width), BF),
        pltpu.VMEM((256, width), BF), pltpu.VMEM((512, width), BF),
        pltpu.VMEM((TOK, width), F32), pltpu.VMEM((256, width), F32),
        pltpu.VMEM((256, 128), BF), pltpu.VMEM((256, 384), F32), pltpu.VMEM((384, 256), BF),
        pltpu.VMEM((256, 384), BF),
        pltpu.VMEM((384, width), BF), pltpu.VMEM((384, width), BF),
        pltpu.VMEM((384, width), BF), pltpu.VMEM((384, width), BF),
        pltpu.VMEM((8, 128), F32), pltpu.VMEM((64, 128), F32),
        pltpu.VMEM((96, 128), F32),
        dma((12,)), dma((8,)), dma((8,)),
        dma((16,)), dma((16,)), dma((16,)), dma((16,)),
        dma((16,)), dma((16,)), dma((16,)), dma((16,)),
        dma((16,)), dma((16,)), dma((8,)), dma((8,)),
        dma((24,)), dma((24,)), dma((24,)), dma((24,)),
        dma((8,)), dma((8,)), dma((12,)), dma((12,)),
    ]
    stream_out, query, new_bias = pl.pallas_call(
        kernel,
        out_shape=(
            jax.ShapeDtypeStruct((TOK, width), BF),
            jax.ShapeDtypeStruct((512, 256), BF),
            jax.ShapeDtypeStruct((1, 64), F32),
        ),
        in_specs=[hbm] * 12,
        out_specs=(vmem, vmem, vmem),
        scratch_shapes=scratch,
        compiler_params=pltpu.CompilerParams(
            collective_id=0, has_side_effects=True, vmem_limit_bytes=60 * 1024 * 1024
        ),
    )(
        attn_heads, w_out, residual, gain_moe.reshape(1, -1), router.T, route_ids.T,
        w_gate, w_up, w_down, bias.reshape(1, -1), gain_next.reshape(1, -1), w_query,
    )
    return stream_out, query, new_bias.reshape(-1)


def solution(mesh):
    in_specs = (
        P(("dp", "fold"), "tensor"),
        P("tensor", None),
        P(("dp", "fold", "tensor"), None),
        P(),
        P(),
        P(("dp", "fold", "tensor"), None),
        P(("fold", "tensor"), None, None),
        P(("fold", "tensor"), None, None),
        P(("fold", "tensor"), None, None),
        P(),
        P(),
        P(None, "tensor"),
    )
    out_specs = (P(("dp", "fold", "tensor"), None), P(("dp", "fold"), "tensor"), P())
    return jax.shard_map(local, mesh=mesh, in_specs=in_specs, out_specs=out_specs, check_vma=False)
```

```python
import math

import jax
import jax.numpy as jnp
from jax import lax
from jax.experimental import pallas as pl
from jax.experimental.pallas import tpu as pltpu
from jax.sharding import PartitionSpec as P

TOK = 32
HALF = 16
WIDE = 1024
CAP = 6
NY = 8
NX = 4
NZ = 12
MEAN_LOAD = 3072.0

REL = (0, -1, 1, -2, 2, -3, 3, 4)
AG_SRC = ((0, 1, 3, 5), (0, 2, 4, 6))
AG_DST = ((1, 3, 5, 7), (2, 4, 6, 7))
RS_BLK = ((7, 6, 4, 2), (7, 5, 3, 1))
TILE_BLOCKS = ((0, 2), (2, 5), (5, 7))

BF = jnp.bfloat16
F32 = jnp.float32


def dot(a, b):
    return jnp.dot(a, b, preferred_element_type=F32)


def kernel(
    attn, w_out, residual_h, gain1_h, router_h, ids_h, w_gate, w_up, w_down, bias_h, gain2_h, w_query,
    stream_out, query, new_bias,
    attn_v, attn_o, w_out_v, wg, wu, wd, wq,
    residual, gain1, router_t, ids_t, bias, gain2,
    part, sib_send, sib_recv,
    rs1_send, rs1_recv, rs2_send, rs2_recv,
    norm, norm2, stream, comb,
    table, pick, pick_t, mix,
    x_send, x_recv, y_send, y_recv,
    cx_send, cx_recv, cz,
    sem_load, s_sib, r_sib,
    s_rs1, r_rs1, s_rs2, r_rs2, s_ag1, r_ag1, s_ag2, r_ag2, s_agc, r_agc, s_tab, r_tab,
    s_x, r_x, s_y, r_y, s_cx, r_cx, s_cz, r_cz,
):
    z = lax.axis_index("dp")
    x = lax.axis_index("fold")
    t = lax.axis_index("tensor")
    y = t // 2
    c = t % 2
    sib = {"tensor": y * 2 + (1 - c)}
    ring = ({"tensor": (t + 2) % 16}, {"tensor": (t + 14) % 16})

    def plane(dx, cr, sign):
        core = c + cr * (1 - 2 * c)
        return {"fold": (x + sign * dx + NX) % NX, "tensor": y * 2 + core}

    pending = []

    def send(src, dst, ss, rs, dev):
        copy = pltpu.make_async_remote_copy(
            src_ref=src, dst_ref=dst, send_sem=ss, recv_sem=rs,
            device_id=dev, device_id_type=pl.DeviceIdType.MESH,
        )
        copy.start()
        pending.append(copy)
        return copy

    def drain(count):
        for copy in pending[:count]:
            copy.wait_send()
        del pending[:count]

    barrier = pltpu.get_barrier_semaphore()
    peers = [sib, ring[0], ring[1]]
    for dx in range(1, NX):
        for cr in range(2):
            peers.append(plane(dx, cr, 1))
    for peer in peers:
        pl.semaphore_signal(barrier, inc=1, device_id=peer, device_id_type=pl.DeviceIdType.MESH)
    for k in range(1, NZ):

        @pl.when(z + k < NZ)
        def _(k=k):
            pl.semaphore_signal(
                barrier, inc=1, device_id={"dp": (z + k) % NZ}, device_id_type=pl.DeviceIdType.MESH
            )

    def load(i, src, dst):
        copy = pltpu.make_async_copy(src, dst, sem_load.at[i])
        copy.start()
        return copy

    load_ids = load(0, ids_h, ids_t)
    load_attn = load(1, attn, attn_v)
    load_w_out = load(2, w_out, w_out_v)
    load_residual = load(3, residual_h, residual)
    load_gain1 = load(4, gain1_h, gain1)
    load_router = load(5, router_h, router_t)

    load_ids.wait()
    expert = lax.broadcasted_iota(jnp.int32, (128, TOK), 0)
    hit = jnp.zeros((128, TOK), F32)
    for k in range(8):
        hit = hit + jnp.where(expert == ids_t[k : k + 1, :], 1.0, 0.0)
    rows = lax.broadcasted_iota(jnp.int32, (TOK, TOK), 0)
    cols = lax.broadcasted_iota(jnp.int32, (TOK, TOK), 1)
    before = dot(hit.astype(BF), jnp.where(rows < cols, 1.0, 0.0).astype(BF))
    slot = jnp.where(hit > 0.5, before, -1.0).astype(BF)
    eye = jnp.where(rows == cols, 1.0, 0.0).astype(BF)
    own_table = lax.dot_general(eye, slot, (((1,), (1,)), ((), ())), preferred_element_type=F32)
    table[0:TOK, :] = own_table.astype(BF)

    def table_send(d, s):
        return send(
            table.at[pl.ds(AG_SRC[d][s] * TOK, TOK), :],
            table.at[pl.ds(AG_DST[d][s] * TOK, TOK), :],
            s_tab.at[d * 4 + s], r_tab.at[d * 4 + s], ring[d],
        )

    load_attn.wait()
    for par in range(2):
        for a in range(8):
            core = c if par == 1 else 1 - c
            row = ((y + REL[a] + NY) % NY * 2 + core) * TOK
            at = (par * 8 + a) * TOK
            attn_o[at : at + TOK, :] = attn_v[pl.ds(pl.multiple_of(row, TOK), TOK), :]
    load_w_out.wait()
    tab = {}
    sib_copies = {}
    for col in range(0, 2048, 512):
        sib_send[:, col : col + 512] = dot(attn_o[0:256, :], w_out_v[:, col : col + 512]).astype(BF)
    pl.semaphore_wait(barrier, len(peers) + z)
    for a in range(7, -1, -1):
        here = pl.ds(a * TOK, TOK)
        sib_copies[a] = send(
            sib_send.at[here, :], sib_recv.at[here, :], s_sib.at[a], r_sib.at[a], sib
        )
    for d in range(2):
        tab[d, 0] = table_send(d, 0)
    for col in range(0, 2048, 512):
        part[:, col : col + 512] = dot(attn_o[256:512, :], w_out_v[:, col : col + 512])
    load_wg = load(6, w_gate.at[0], wg)
    load_wu = load(7, w_up.at[0], wu)
    load_wd = load(8, w_down.at[0], wd)
    load_wq = load(9, w_query, wq)
    load_bias = load(10, bias_h, bias)
    load_gain2 = load(11, gain2_h, gain2)

    def rs_step(s, own, send_buf, recv_buf, ss, rs, copies):
        order = ((0, 0), (1, 1)) if s == 0 else ((0, 1), (1, 0), (0, 0), (1, 1))
        for first in range(0, len(order), 2):
            for q in range(2):
                for d, h in order[first : first + 2]:
                    idx = d * 8 + s * 2 + h
                    value = own(RS_BLK[d][s], h, q)
                    if (d, s - 1, h, q) in copies:
                        copies[d, s - 1, h, q].wait_recv()
                        prev = (idx - 2) * HALF
                        value = value + recv_buf[q, prev : prev + HALF, :].astype(F32)
                    here = pl.ds(idx * HALF, HALF)
                    send_buf[q, idx * HALF : (idx + 1) * HALF, :] = value.astype(BF)
                    copies[d, s, h, q] = send(
                        send_buf.at[q, here, :], recv_buf.at[q, here, :],
                        ss.at[idx * 2 + q], rs.at[idx * 2 + q], ring[d],
                    )

    def rs_last(h, own, recv_buf, copies):
        values = []
        for q in range(2):
            value = own(0, h, q)
            for d in range(2):
                copies[d, 3, h, q].wait_recv()
                at = (d * 8 + 6 + h) * HALF
                value = value + recv_buf[q, at : at + HALF, :].astype(F32)
            values.append(value)
        return jnp.concatenate(values, axis=1)

    def own1(a, h, q):
        at, col = a * TOK + h * HALF, q * WIDE
        return part[at : at + HALF, col : col + WIDE] + sib_recv[
            at : at + HALF, col : col + WIDE
        ].astype(F32)

    sib_here = set()

    def sib_wait(*blocks):
        for a in blocks:
            if a not in sib_here:
                sib_here.add(a)
                sib_copies[a].wait_recv()

    rs1 = {}
    for s in range(3):
        sib_wait(RS_BLK[0][s], RS_BLK[1][s])
        rs_step(s, own1, rs1_send, rs1_recv, s_rs1, r_rs1, rs1)
        for d in range(2):
            tab[d, s].wait_recv()
            if s < 2 or d == 0:
                tab[d, s + 1] = table_send(d, s + 1)
    sib_wait(2, 1, 0)
    rs_step(3, own1, rs1_send, rs1_recv, s_rs1, r_rs1, rs1)
    tab[0, 3].wait_recv()

    all_slots = table[...].astype(F32)
    count = jnp.sum(jnp.where(all_slots > -0.5, 1.0, 0.0), axis=0, keepdims=True)
    cx_send[...] = jnp.broadcast_to(count, (8, 128))
    cx = []
    for dest in range(1, 8):
        cx.append(
            send(
                cx_send, cx_recv.at[pl.ds(dest * 8, 8), :],
                s_cx.at[dest], r_cx.at[dest], plane(dest // 2, dest % 2, 1),
            )
        )

    e_at = lax.broadcasted_iota(jnp.int32, (128, 384), 0)
    r_at = lax.broadcasted_iota(jnp.int32, (128, 384), 1)
    dest_at = (r_at >> 4) & 7
    cr_at = dest_at & 1
    e_of = ((x + (dest_at >> 1)) & 3) * 16 + y * 2 + c + cr_at * (1 - 2 * c)
    select = jnp.where(e_at == e_of, 1.0, 0.0).astype(BF)
    r_row = lax.broadcasted_iota(jnp.int32, (256, 384), 1)
    packed = (r_row >> 7) * 16 + (r_row & 15)
    block_of = (packed * 43) >> 8
    slot_of = (packed - block_of * 6).astype(F32)
    tok_block = lax.broadcasted_iota(jnp.int32, (256, 384), 0) >> 5
    spread = dot(table[...], select)
    match = jnp.logical_and(spread == slot_of, tok_block == block_of)
    pick[...] = jnp.where(match, 1.0, 0.0)
    pick_t[...] = pick[...].T.astype(BF)
    load_residual.wait()
    load_gain1.wait()

    def normalize(value, gain):
        mean_sq = jnp.mean(value * value, axis=-1, keepdims=True)
        return (value * lax.rsqrt(mean_sq + 1e-06) * gain[...]).astype(BF)

    def ag_send(buf, scale, d, s, h, ss, rs):
        src = AG_SRC[d][s] * scale + h * HALF
        dst = AG_DST[d][s] * scale + h * HALF
        idx = d * 8 + s * 2 + h
        return send(
            buf.at[pl.ds(src, HALF), :], buf.at[pl.ds(dst, HALF), :], ss.at[idx], rs.at[idx], ring[d]
        )

    ag1 = {}
    for h in range(2):
        at = h * HALF
        value = residual[at : at + HALF, :].astype(F32) + rs_last(h, own1, rs1_recv, rs1)
        stream[at : at + HALF, :] = value
        norm[at : at + HALF, :] = normalize(value, gain1)
        for d in range(2):
            ag1[d, 0, h] = ag_send(norm, TOK, d, 0, h, s_ag1, r_ag1)

    def ag1_pass(s):
        for h in range(2):
            for d in range(2):
                if (d, s, h) not in ag1:
                    continue
                ag1[d, s, h].wait_recv()
                if s < 2 or (s == 2 and h == d):
                    ag1[d, s + 1, h] = ag_send(norm, TOK, d, s + 1, h, s_ag1, r_ag1)

    xs = {}

    def dispatch(g):
        lo, hi = TILE_BLOCKS[g][0] * TOK, (TILE_BLOCKS[g][1] + 1) * TOK
        lhs = pick_t[g * 128 : (g + 1) * 128, lo:hi]
        for col in range(0, 2048, 512):
            x_send[g * 128 : (g + 1) * 128, col : col + 512] = dot(
                lhs, norm[lo:hi, col : col + 512]
            ).astype(BF)
        for dest in (4, 5, 2, 3, 6, 7, 1):
            at = pl.ds(g * 128 + dest * HALF, HALF)
            xs[g, dest] = send(
                x_send.at[at, :], x_recv.at[at, :],
                s_x.at[g * 8 + dest], r_x.at[g * 8 + dest], plane(dest // 2, dest % 2, 1),
            )
        x_recv[g * 128 : g * 128 + HALF, :] = x_send[g * 128 : g * 128 + HALF, :]

    def z_copy(k):
        return pltpu.make_async_remote_copy(
            src_ref=cz.at[pl.ds(0, 8), :], dst_ref=cz.at[pl.ds(k * 8, 8), :],
            send_sem=s_cz.at[k], recv_sem=r_cz.at[k],
            device_id={"dp": (z + NZ - k) % NZ}, device_id_type=pl.DeviceIdType.MESH,
        )

    def z_each(cond, act):
        for k in range(1, NZ):

            @pl.when(cond(k))
            def _(k=k):
                act(z_copy(k))

    ag1_pass(0)
    dispatch(0)
    ag1_pass(1)
    ag1_pass(2)
    dispatch(1)
    total = cx_send[...]
    for dest in range(1, 8):
        cx[dest - 1].wait_recv()
        total = total + cx_recv[dest * 8 : dest * 8 + 8, :]
    cz[0:8, :] = total
    z_each(lambda k: k <= z, lambda copy: copy.start())
    ag1_pass(3)
    dispatch(2)
    load_router.wait()

    logits = lax.dot_general(
        norm[...], router_t[...], (((1,), (1,)), ((), ())), preferred_element_type=F32
    )
    score = 1.0 / (1.0 + jnp.exp(-logits))
    score = jnp.where(table[:, 0:64].astype(F32) > -0.5, score, 0.0)
    weight = (score / jnp.sum(score, axis=1, keepdims=True)).astype(BF)
    mix[...] = (dot(weight, select[0:64, :]) * pick[...]).astype(BF)

    load_wg.wait()
    load_wu.wait()
    load_wd.wait()
    ys = {}

    def give_back(g, dests):
        for dest in dests:
            at = pl.ds(g * 128 + dest * HALF, HALF)
            ys[g, dest] = send(
                y_send.at[at, :], y_recv.at[at, :],
                s_y.at[g * 8 + dest], r_y.at[g * 8 + dest], plane(dest // 2, dest % 2, -1),
            )

    for g in range(3):
        for dest in (2, 3, 6, 7, 4, 5, 1):
            xs[g, dest].wait_recv()
        if g == 2:
            give_back(0, (2, 3, 6, 7))
        arrived = x_recv[g * 128 : (g + 1) * 128, :]
        gate = dot(arrived, wg[...])
        upper = dot(arrived, wu[...])
        act = (gate / (1.0 + jnp.exp(-gate)) * upper).astype(BF)
        for col in range(0, 2048, 512):
            y_send[g * 128 : (g + 1) * 128, col : col + 512] = dot(
                act, wd[:, col : col + 512]
            ).astype(BF)

    sent = len(pending)
    give_back(2, (4, 5, 2, 3, 6, 7, 1))
    give_back(1, (4, 5, 2, 3, 6, 7, 1))
    give_back(0, (4, 5, 1))
    for g in range(3):
        y_recv[g * 128 : g * 128 + HALF, :] = y_send[g * 128 : g * 128 + HALF, :]
    z_each(lambda k: z + k < NZ, lambda copy: copy.wait_recv())
    z_each(lambda k: k > z, lambda copy: copy.start())
    drain(sent)

    def own2(a, h, q):
        at, col = a * TOK + h * HALF, q * WIDE
        return comb[at : at + HALF, col : col + WIDE]

    def mixdown(g):
        for dest in (2, 3, 6, 7, 4, 5, 1):
            ys[g, dest].wait_recv()
        lo, hi = TILE_BLOCKS[g][0] * TOK, (TILE_BLOCKS[g][1] + 1) * TOK
        for col in range(0, 2048, 512):
            value = dot(
                mix[lo:hi, g * 128 : (g + 1) * 128],
                y_recv[g * 128 : (g + 1) * 128, col : col + 512],
            )
            if g == 2:
                comb[lo:hi, col : col + 512] = value
            else:
                comb[lo : hi - TOK, col : col + 512] = value[: hi - TOK - lo, :]
                comb[hi - TOK : hi, col : col + 512] += value[hi - TOK - lo :, :]

    rs2 = {}
    mixdown(2)
    rs_step(0, own2, rs2_send, rs2_recv, s_rs2, r_rs2, rs2)
    mixdown(1)
    rs_step(1, own2, rs2_send, rs2_recv, s_rs2, r_rs2, rs2)
    rs_step(2, own2, rs2_send, rs2_recv, s_rs2, r_rs2, rs2)
    mixdown(0)
    rs_step(3, own2, rs2_send, rs2_recv, s_rs2, r_rs2, rs2)

    z_each(lambda k: z + k >= NZ, lambda copy: copy.wait_recv())
    total = cz[0:1, :]
    for dz in range(1, NZ):
        total = total + cz[dz * 8 : dz * 8 + 1, :]
    load_bias.wait()
    new_bias[...] = bias[...] + 0.5 * (MEAN_LOAD - total[:, 0:64]) / math.sqrt(MEAN_LOAD)
    load_gain2.wait()
    for k in range(1, NZ):
        z_copy(k).wait_send()

    ag2 = {}
    agc = {}

    def ag2_send(d, s, h, q):
        src = AG_SRC[d][s] * 2 * TOK + h * HALF
        dst = AG_DST[d][s] * 2 * TOK + h * HALF
        idx = (d * 8 + s * 2 + h) * 2 + q
        ag2[d, s, h, q] = send(
            norm2.at[q, pl.ds(src, HALF), :], norm2.at[q, pl.ds(dst, HALF), :],
            s_ag2.at[idx], r_ag2.at[idx], ring[d],
        )

    def share(a, h, q):
        src = pl.ds(a * 2 * TOK + h * HALF, HALF)
        dst = pl.ds((a * 2 + 1) * TOK + h * HALF, HALF)
        idx = (a * 2 + h) * 2 + q
        agc[a, h, q] = send(
            norm2.at[q, src, :], norm2.at[q, dst, :], s_agc.at[idx], r_agc.at[idx], sib
        )

    sent = len(pending)
    for h in range(2):
        at = h * HALF
        value = stream[at : at + HALF, :] + rs_last(h, own2, rs2_recv, rs2)
        scaled = normalize(value, gain2)
        for q in range(2):
            norm2[q, at : at + HALF, :] = scaled[:, q * WIDE : (q + 1) * WIDE]
            for d in range(2):
                ag2_send(d, 0, h, q)
        stream_out[at : at + HALF, :] = value.astype(BF)
    for h in range(2):
        for q in range(2):
            share(0, h, q)
    drain(sent)

    def ag2_pass(s):
        for h in range(2):
            for q in range(2):
                for d in range(2):
                    if (d, s, h, q) not in ag2:
                        continue
                    ag2[d, s, h, q].wait_recv()
                    if s < 2 or (s == 2 and h == d):
                        ag2_send(d, s + 1, h, q)
                    share(AG_DST[d][s], h, q)

    def project(first, last):
        for a in range(first, last + 1):
            for h in range(2):
                for q in range(2):
                    agc[a, h, q].wait_recv()
        lo, hi = first * 2 * TOK, (last + 1) * 2 * TOK
        value = dot(norm2[0, lo:hi, :], wq[0:WIDE, :]) + dot(norm2[1, lo:hi, :], wq[WIDE:, :])
        value = value.astype(BF)
        for a in range(first, last + 1):
            for par in range(2):
                core = c if par == 0 else 1 - c
                row = ((y + REL[a] + NY) % NY * 2 + core) * TOK
                at = ((a - first) * 2 + par) * TOK
                query[pl.ds(pl.multiple_of(row, TOK), TOK), :] = value[at : at + TOK, :]

    load_wq.wait()
    ag2_pass(0)
    project(0, 0)
    ag2_pass(1)
    project(1, 2)
    ag2_pass(2)
    project(3, 4)
    project(5, 6)
    ag2_pass(3)
    project(7, 7)

    drain(len(pending))


def local(
    attn_heads, w_out, residual, gain_moe, router, route_ids,
    w_gate, w_up, w_down, bias, gain_next, w_query,
):
    width = residual.shape[1]
    vmem = pl.BlockSpec(memory_space=pltpu.VMEM)
    hbm = pl.BlockSpec(memory_space=pl.ANY)
    dma = pltpu.SemaphoreType.DMA
    scratch = [
        pltpu.VMEM((512, 256), BF), pltpu.VMEM((512, 256), BF), pltpu.VMEM((256, 2048), BF),
        pltpu.VMEM((2048, 768), BF), pltpu.VMEM((2048, 768), BF),
        pltpu.VMEM((768, 2048), BF), pltpu.VMEM((2048, 256), BF),
        pltpu.VMEM((TOK, width), BF), pltpu.VMEM((1, width), F32), pltpu.VMEM((64, width), BF),
        pltpu.VMEM((8, TOK), jnp.int32), pltpu.VMEM((1, 64), F32), pltpu.VMEM((1, width), F32),
        pltpu.VMEM((256, width), F32), pltpu.VMEM((256, width), BF), pltpu.VMEM((256, width), BF),
        pltpu.VMEM((2, 256, WIDE), BF), pltpu.VMEM((2, 256, WIDE), BF),
        pltpu.VMEM((2, 256, WIDE), BF), pltpu.VMEM((2, 256, WIDE), BF),
        pltpu.VMEM((256, width), BF), pltpu.VMEM((2, 512, WIDE), BF),
        pltpu.VMEM((TOK, width), F32), pltpu.VMEM((256, width), F32),
        pltpu.VMEM((256, 128), BF), pltpu.VMEM((256, 384), F32), pltpu.VMEM((384, 256), BF),
        pltpu.VMEM((256, 384), BF),
        pltpu.VMEM((384, width), BF), pltpu.VMEM((384, width), BF),
        pltpu.VMEM((384, width), BF), pltpu.VMEM((384, width), BF),
        pltpu.VMEM((8, 128), F32), pltpu.VMEM((64, 128), F32),
        pltpu.VMEM((96, 128), F32),
        dma((12,)), dma((8,)), dma((8,)),
        dma((32,)), dma((32,)), dma((32,)), dma((32,)),
        dma((16,)), dma((16,)), dma((32,)), dma((32,)),
        dma((32,)), dma((32,)), dma((8,)), dma((8,)),
        dma((24,)), dma((24,)), dma((24,)), dma((24,)),
        dma((8,)), dma((8,)), dma((12,)), dma((12,)),
    ]
    stream_out, query, new_bias = pl.pallas_call(
        kernel,
        out_shape=(
            jax.ShapeDtypeStruct((TOK, width), BF),
            jax.ShapeDtypeStruct((512, 256), BF),
            jax.ShapeDtypeStruct((1, 64), F32),
        ),
        in_specs=[hbm] * 12,
        out_specs=(vmem, vmem, vmem),
        scratch_shapes=scratch,
        compiler_params=pltpu.CompilerParams(
            collective_id=0, has_side_effects=True, vmem_limit_bytes=60 * 1024 * 1024
        ),
    )(
        attn_heads, w_out, residual, gain_moe.reshape(1, -1), router.T, route_ids.T,
        w_gate, w_up, w_down, bias.reshape(1, -1), gain_next.reshape(1, -1), w_query,
    )
    return stream_out, query, new_bias.reshape(-1)


def solution(mesh):
    in_specs = (
        P(("dp", "fold"), "tensor"),
        P("tensor", None),
        P(("dp", "fold", "tensor"), None),
        P(),
        P(),
        P(("dp", "fold", "tensor"), None),
        P(("fold", "tensor"), None, None),
        P(("fold", "tensor"), None, None),
        P(("fold", "tensor"), None, None),
        P(),
        P(),
        P(None, "tensor"),
    )
    out_specs = (P(("dp", "fold", "tensor"), None), P(("dp", "fold"), "tensor"), P())
    return jax.shard_map(local, mesh=mesh, in_specs=in_specs, out_specs=out_specs, check_vma=False)
```

```python
import math

import jax
import jax.numpy as jnp
from jax import lax
from jax.experimental import pallas as pl
from jax.experimental.pallas import tpu as pltpu
from jax.sharding import PartitionSpec as P

TOK = 32
HALF = 16
WIDE = 1024
CAP = 6
NY = 8
NX = 4
NZ = 12
MEAN_LOAD = 3072.0

REL = (0, -1, 1, -2, 2, -3, 3, 4)
AG_SRC = ((0, 1, 3, 5), (0, 2, 4, 6))
AG_DST = ((1, 3, 5, 7), (2, 4, 6, 7))
RS_BLK = ((7, 6, 4, 2), (7, 5, 3, 1))
TILE_BLOCKS = ((0, 2), (2, 5), (5, 7))

BF = jnp.bfloat16
F32 = jnp.float32


def dot(a, b):
    return jnp.dot(a, b, preferred_element_type=F32)


def kernel(
    attn, w_out, residual_h, gain1_h, router_h, ids_h, w_gate, w_up, w_down, bias_h, gain2_h, w_query,
    stream_out, query, new_bias,
    attn_v, attn_o, w_out_v, wg, wu, wd, wq,
    residual, gain1, router_t, ids_t, bias, gain2,
    part, sib_send, sib_recv,
    rs1_send, rs1_recv, rs2_send, rs2_recv,
    norm, norm2, stream, comb,
    table, pick, pick_t, mix,
    x_send, x_recv, y_send, y_recv,
    cx_send, cx_recv, cz,
    sem_load, s_sib, r_sib,
    s_rs1, r_rs1, s_rs2, r_rs2, s_ag1, r_ag1, s_ag2, r_ag2, s_agc, r_agc, s_tab, r_tab,
    s_x, r_x, s_y, r_y, s_cx, r_cx, s_cz, r_cz,
):
    z = lax.axis_index("dp")
    x = lax.axis_index("fold")
    t = lax.axis_index("tensor")
    y = t // 2
    c = t % 2
    sib = {"tensor": y * 2 + (1 - c)}
    ring = ({"tensor": (t + 2) % 16}, {"tensor": (t + 14) % 16})

    def plane(dx, cr, sign):
        core = c + cr * (1 - 2 * c)
        return {"fold": (x + sign * dx + NX) % NX, "tensor": y * 2 + core}

    pending = []

    def send(src, dst, ss, rs, dev):
        copy = pltpu.make_async_remote_copy(
            src_ref=src, dst_ref=dst, send_sem=ss, recv_sem=rs,
            device_id=dev, device_id_type=pl.DeviceIdType.MESH,
        )
        copy.start()
        pending.append(copy)
        return copy

    def drain(count):
        for copy in pending[:count]:
            copy.wait_send()
        del pending[:count]

    barrier = pltpu.get_barrier_semaphore()
    peers = [sib, ring[0], ring[1]]
    for dx in range(1, NX):
        for cr in range(2):
            peers.append(plane(dx, cr, 1))
    for peer in peers:
        pl.semaphore_signal(barrier, inc=1, device_id=peer, device_id_type=pl.DeviceIdType.MESH)
    for k in range(1, NZ):

        @pl.when(z + k < NZ)
        def _(k=k):
            pl.semaphore_signal(
                barrier, inc=1, device_id={"dp": (z + k) % NZ}, device_id_type=pl.DeviceIdType.MESH
            )

    def load(i, src, dst):
        copy = pltpu.make_async_copy(src, dst, sem_load.at[i])
        copy.start()
        return copy

    load_ids = load(0, ids_h, ids_t)
    load_attn = load(1, attn, attn_v)
    load_w_out = load(2, w_out, w_out_v)
    load_residual = load(3, residual_h, residual)
    load_gain1 = load(4, gain1_h, gain1)
    load_router = load(5, router_h, router_t)

    load_ids.wait()
    expert = lax.broadcasted_iota(jnp.int32, (128, TOK), 0)
    hit = jnp.zeros((128, TOK), F32)
    for k in range(8):
        hit = hit + jnp.where(expert == ids_t[k : k + 1, :], 1.0, 0.0)
    rows = lax.broadcasted_iota(jnp.int32, (TOK, TOK), 0)
    cols = lax.broadcasted_iota(jnp.int32, (TOK, TOK), 1)
    before = dot(hit.astype(BF), jnp.where(rows < cols, 1.0, 0.0).astype(BF))
    slot = jnp.where(hit > 0.5, before, -1.0).astype(BF)
    eye = jnp.where(rows == cols, 1.0, 0.0).astype(BF)
    own_table = lax.dot_general(eye, slot, (((1,), (1,)), ((), ())), preferred_element_type=F32)
    table[0:TOK, :] = own_table.astype(BF)

    def table_send(d, s):
        return send(
            table.at[pl.ds(AG_SRC[d][s] * TOK, TOK), :],
            table.at[pl.ds(AG_DST[d][s] * TOK, TOK), :],
            s_tab.at[d * 4 + s], r_tab.at[d * 4 + s], ring[d],
        )

    load_attn.wait()
    for par in range(2):
        for a in range(8):
            core = c if par == 1 else 1 - c
            row = ((y + REL[a] + NY) % NY * 2 + core) * TOK
            at = (par * 8 + a) * TOK
            attn_o[at : at + TOK, :] = attn_v[pl.ds(pl.multiple_of(row, TOK), TOK), :]
    load_w_out.wait()
    tab = {}
    sib_copies = {}
    for col in range(0, 2048, 512):
        sib_send[:, col : col + 512] = dot(attn_o[0:256, :], w_out_v[:, col : col + 512]).astype(BF)
    pl.semaphore_wait(barrier, len(peers) + z)
    for a in range(7, -1, -1):
        here = pl.ds(a * TOK, TOK)
        sib_copies[a] = send(
            sib_send.at[here, :], sib_recv.at[here, :], s_sib.at[a], r_sib.at[a], sib
        )
    for d in range(2):
        tab[d, 0] = table_send(d, 0)
    for col in range(0, 2048, 512):
        part[:, col : col + 512] = dot(attn_o[256:512, :], w_out_v[:, col : col + 512])
    load_wg = load(6, w_gate.at[0], wg)
    load_wu = load(7, w_up.at[0], wu)
    load_wd = load(8, w_down.at[0], wd)
    load_wq = load(9, w_query, wq)
    load_bias = load(10, bias_h, bias)
    load_gain2 = load(11, gain2_h, gain2)

    def rs_step(s, own, send_buf, recv_buf, ss, rs, copies, upper_first=False):
        order = ((0, 0), (1, 1)) if s == 0 else ((0, 1), (1, 0), (0, 0), (1, 1))
        if upper_first:
            order = ((0, 0), (1, 0), (0, 1), (1, 1))
        for first in range(0, len(order), 2):
            for q in range(2):
                for d, h in order[first : first + 2]:
                    idx = d * 8 + s * 2 + h
                    value = own(RS_BLK[d][s], h, q)
                    if (d, s - 1, h, q) in copies:
                        copies[d, s - 1, h, q].wait_recv()
                        prev = (idx - 2) * HALF
                        value = value + recv_buf[q, prev : prev + HALF, :].astype(F32)
                    here = pl.ds(idx * HALF, HALF)
                    send_buf[q, idx * HALF : (idx + 1) * HALF, :] = value.astype(BF)
                    copies[d, s, h, q] = send(
                        send_buf.at[q, here, :], recv_buf.at[q, here, :],
                        ss.at[idx * 2 + q], rs.at[idx * 2 + q], ring[d],
                    )

    def rs_last(h, own, recv_buf, copies):
        values = []
        for q in range(2):
            value = own(0, h, q)
            for d in range(2):
                copies[d, 3, h, q].wait_recv()
                at = (d * 8 + 6 + h) * HALF
                value = value + recv_buf[q, at : at + HALF, :].astype(F32)
            values.append(value)
        return jnp.concatenate(values, axis=1)

    def own1(a, h, q):
        at, col = a * TOK + h * HALF, q * WIDE
        return part[at : at + HALF, col : col + WIDE] + sib_recv[
            at : at + HALF, col : col + WIDE
        ].astype(F32)

    sib_here = set()

    def sib_wait(*blocks):
        for a in blocks:
            if a not in sib_here:
                sib_here.add(a)
                sib_copies[a].wait_recv()

    rs1 = {}
    for s in range(3):
        sib_wait(RS_BLK[0][s], RS_BLK[1][s])
        rs_step(s, own1, rs1_send, rs1_recv, s_rs1, r_rs1, rs1)
        for d in range(2):
            tab[d, s].wait_recv()
            if s < 2 or d == 0:
                tab[d, s + 1] = table_send(d, s + 1)
    sib_wait(2, 1, 0)
    rs_step(3, own1, rs1_send, rs1_recv, s_rs1, r_rs1, rs1)
    tab[0, 3].wait_recv()

    all_slots = table[...].astype(F32)
    count = jnp.sum(jnp.where(all_slots > -0.5, 1.0, 0.0), axis=0, keepdims=True)
    cx_send[...] = jnp.broadcast_to(count, (8, 128))
    cx = []
    for dest in range(1, 8):
        cx.append(
            send(
                cx_send, cx_recv.at[pl.ds(dest * 8, 8), :],
                s_cx.at[dest], r_cx.at[dest], plane(dest // 2, dest % 2, 1),
            )
        )

    e_at = lax.broadcasted_iota(jnp.int32, (128, 384), 0)
    r_at = lax.broadcasted_iota(jnp.int32, (128, 384), 1)
    dest_at = (r_at >> 4) & 7
    cr_at = dest_at & 1
    e_of = ((x + (dest_at >> 1)) & 3) * 16 + y * 2 + c + cr_at * (1 - 2 * c)
    select = jnp.where(e_at == e_of, 1.0, 0.0).astype(BF)
    r_row = lax.broadcasted_iota(jnp.int32, (256, 384), 1)
    packed = (r_row >> 7) * 16 + (r_row & 15)
    block_of = (packed * 43) >> 8
    slot_of = (packed - block_of * 6).astype(F32)
    tok_block = lax.broadcasted_iota(jnp.int32, (256, 384), 0) >> 5
    spread = dot(table[...], select)
    match = jnp.logical_and(spread == slot_of, tok_block == block_of)
    pick[...] = jnp.where(match, 1.0, 0.0)
    pick_t[...] = pick[...].T.astype(BF)
    load_residual.wait()
    load_gain1.wait()

    def normalize(value, gain):
        mean_sq = jnp.mean(value * value, axis=-1, keepdims=True)
        return (value * lax.rsqrt(mean_sq + 1e-06) * gain[...]).astype(BF)

    def ag_send(buf, scale, d, s, h, ss, rs):
        src = AG_SRC[d][s] * scale + h * HALF
        dst = AG_DST[d][s] * scale + h * HALF
        idx = d * 8 + s * 2 + h
        return send(
            buf.at[pl.ds(src, HALF), :], buf.at[pl.ds(dst, HALF), :], ss.at[idx], rs.at[idx], ring[d]
        )

    ag1 = {}
    for h in range(2):
        at = h * HALF
        value = residual[at : at + HALF, :].astype(F32) + rs_last(h, own1, rs1_recv, rs1)
        stream[at : at + HALF, :] = value
        norm[at : at + HALF, :] = normalize(value, gain1)
        for d in range(2):
            ag1[d, 0, h] = ag_send(norm, TOK, d, 0, h, s_ag1, r_ag1)

    def ag1_pass(s):
        for h in range(2):
            for d in range(2):
                if (d, s, h) not in ag1:
                    continue
                ag1[d, s, h].wait_recv()
                if s < 2 or (s == 2 and h == d):
                    ag1[d, s + 1, h] = ag_send(norm, TOK, d, s + 1, h, s_ag1, r_ag1)

    xs = {}

    def dispatch(g):
        lo, hi = TILE_BLOCKS[g][0] * TOK, (TILE_BLOCKS[g][1] + 1) * TOK
        lhs = pick_t[g * 128 : (g + 1) * 128, lo:hi]
        for col in range(0, 2048, 512):
            x_send[g * 128 : (g + 1) * 128, col : col + 512] = dot(
                lhs, norm[lo:hi, col : col + 512]
            ).astype(BF)
        for dest in (4, 5, 2, 3, 6, 7, 1):
            at = pl.ds(g * 128 + dest * HALF, HALF)
            xs[g, dest] = send(
                x_send.at[at, :], x_recv.at[at, :],
                s_x.at[g * 8 + dest], r_x.at[g * 8 + dest], plane(dest // 2, dest % 2, 1),
            )
        x_recv[g * 128 : g * 128 + HALF, :] = x_send[g * 128 : g * 128 + HALF, :]

    def z_copy(k):
        return pltpu.make_async_remote_copy(
            src_ref=cz.at[pl.ds(0, 8), :], dst_ref=cz.at[pl.ds(k * 8, 8), :],
            send_sem=s_cz.at[k], recv_sem=r_cz.at[k],
            device_id={"dp": (z + NZ - k) % NZ}, device_id_type=pl.DeviceIdType.MESH,
        )

    def z_each(cond, act):
        for k in range(1, NZ):

            @pl.when(cond(k))
            def _(k=k):
                act(z_copy(k))

    ag1_pass(0)
    dispatch(0)
    ag1_pass(1)
    ag1_pass(2)
    dispatch(1)
    total = cx_send[...]
    for dest in range(1, 8):
        cx[dest - 1].wait_recv()
        total = total + cx_recv[dest * 8 : dest * 8 + 8, :]
    cz[0:8, :] = total
    z_each(lambda k: k <= z, lambda copy: copy.start())
    ag1_pass(3)
    dispatch(2)
    load_router.wait()

    logits = lax.dot_general(
        norm[...], router_t[...], (((1,), (1,)), ((), ())), preferred_element_type=F32
    )
    score = 1.0 / (1.0 + jnp.exp(-logits))
    score = jnp.where(table[:, 0:64].astype(F32) > -0.5, score, 0.0)
    weight = (score / jnp.sum(score, axis=1, keepdims=True)).astype(BF)
    mix[...] = (dot(weight, select[0:64, :]) * pick[...]).astype(BF)

    load_wg.wait()
    load_wu.wait()
    load_wd.wait()
    ys = {}

    def give_back(g, dests):
        for dest in dests:
            at = pl.ds(g * 128 + dest * HALF, HALF)
            ys[g, dest] = send(
                y_send.at[at, :], y_recv.at[at, :],
                s_y.at[g * 8 + dest], r_y.at[g * 8 + dest], plane(dest // 2, dest % 2, -1),
            )

    for g in range(3):
        if g == 2:
            gone = [xs[2, dest] for dest in range(1, 8)]
            for copy in gone:
                copy.wait_send()
            pending[:] = [copy for copy in pending if all(copy is not other for other in gone)]
            give_back(0, (2, 3, 6, 7, 4))
        for dest in (2, 3, 6, 7, 4, 5, 1):
            xs[g, dest].wait_recv()
        arrived = x_recv[g * 128 : (g + 1) * 128, :]
        gate = dot(arrived, wg[...])
        upper = dot(arrived, wu[...])
        act = (gate / (1.0 + jnp.exp(-gate)) * upper).astype(BF)
        for col in range(0, 2048, 512):
            y_send[g * 128 : (g + 1) * 128, col : col + 512] = dot(
                act, wd[:, col : col + 512]
            ).astype(BF)

    sent = len(pending)
    give_back(2, (4, 5, 2, 3, 6, 7, 1))
    give_back(1, (4, 5, 2, 3, 6, 7, 1))
    give_back(0, (5, 1))
    for g in range(3):
        y_recv[g * 128 : g * 128 + HALF, :] = y_send[g * 128 : g * 128 + HALF, :]
    z_each(lambda k: z + k < NZ, lambda copy: copy.wait_recv())
    z_each(lambda k: k > z, lambda copy: copy.start())
    drain(sent)

    def own2(a, h, q):
        at, col = a * TOK + h * HALF, q * WIDE
        return comb[at : at + HALF, col : col + WIDE]

    def mixdown(g):
        for dest in (2, 3, 6, 7, 4, 5, 1):
            ys[g, dest].wait_recv()
        lo, hi = TILE_BLOCKS[g][0] * TOK, (TILE_BLOCKS[g][1] + 1) * TOK
        for col in range(0, 2048, 512):
            value = dot(
                mix[lo:hi, g * 128 : (g + 1) * 128],
                y_recv[g * 128 : (g + 1) * 128, col : col + 512],
            )
            if g == 2:
                comb[lo:hi, col : col + 512] = value
            else:
                comb[lo : hi - TOK, col : col + 512] = value[: hi - TOK - lo, :]
                comb[hi - TOK : hi, col : col + 512] += value[hi - TOK - lo :, :]

    rs2 = {}
    mixdown(2)
    rs_step(0, own2, rs2_send, rs2_recv, s_rs2, r_rs2, rs2)
    mixdown(1)
    rs_step(1, own2, rs2_send, rs2_recv, s_rs2, r_rs2, rs2)
    rs_step(2, own2, rs2_send, rs2_recv, s_rs2, r_rs2, rs2)
    mixdown(0)
    rs_step(3, own2, rs2_send, rs2_recv, s_rs2, r_rs2, rs2, upper_first=True)

    z_each(lambda k: z + k >= NZ, lambda copy: copy.wait_recv())
    total = cz[0:1, :]
    for dz in range(1, NZ):
        total = total + cz[dz * 8 : dz * 8 + 1, :]
    load_bias.wait()
    new_bias[...] = bias[...] + 0.5 * (MEAN_LOAD - total[:, 0:64]) / math.sqrt(MEAN_LOAD)
    load_gain2.wait()
    for k in range(1, NZ):
        z_copy(k).wait_send()

    ag2 = {}
    agc = {}

    def ag2_send(d, s, h, q):
        src = AG_SRC[d][s] * 2 * TOK + h * HALF
        dst = AG_DST[d][s] * 2 * TOK + h * HALF
        idx = (d * 8 + s * 2 + h) * 2 + q
        ag2[d, s, h, q] = send(
            norm2.at[q, pl.ds(src, HALF), :], norm2.at[q, pl.ds(dst, HALF), :],
            s_ag2.at[idx], r_ag2.at[idx], ring[d],
        )

    def share(a, h, q):
        src = pl.ds(a * 2 * TOK + h * HALF, HALF)
        dst = pl.ds((a * 2 + 1) * TOK + h * HALF, HALF)
        idx = (a * 2 + h) * 2 + q
        agc[a, h, q] = send(
            norm2.at[q, src, :], norm2.at[q, dst, :], s_agc.at[idx], r_agc.at[idx], sib
        )

    sent = len(pending)
    for h in range(2):
        at = h * HALF
        value = stream[at : at + HALF, :] + rs_last(h, own2, rs2_recv, rs2)
        scaled = normalize(value, gain2)
        for q in range(2):
            norm2[q, at : at + HALF, :] = scaled[:, q * WIDE : (q + 1) * WIDE]
            for d in range(2):
                ag2_send(d, 0, h, q)
        stream_out[at : at + HALF, :] = value.astype(BF)
    for h in range(2):
        for q in range(2):
            share(0, h, q)
    drain(sent)

    def ag2_pass(s):
        for h in range(2):
            for q in range(2):
                for d in range(2):
                    if (d, s, h, q) not in ag2:
                        continue
                    ag2[d, s, h, q].wait_recv()
                    if s < 2 or (s == 2 and h == d):
                        ag2_send(d, s + 1, h, q)
                    share(AG_DST[d][s], h, q)

    def project(first, last):
        for a in range(first, last + 1):
            for h in range(2):
                for q in range(2):
                    agc[a, h, q].wait_recv()
        lo, hi = first * 2 * TOK, (last + 1) * 2 * TOK
        value = dot(norm2[0, lo:hi, :], wq[0:WIDE, :]) + dot(norm2[1, lo:hi, :], wq[WIDE:, :])
        value = value.astype(BF)
        for a in range(first, last + 1):
            for par in range(2):
                core = c if par == 0 else 1 - c
                row = ((y + REL[a] + NY) % NY * 2 + core) * TOK
                at = ((a - first) * 2 + par) * TOK
                query[pl.ds(pl.multiple_of(row, TOK), TOK), :] = value[at : at + TOK, :]

    load_wq.wait()
    ag2_pass(0)
    project(0, 0)
    ag2_pass(1)
    project(1, 2)
    ag2_pass(2)
    project(3, 4)
    project(5, 6)
    ag2_pass(3)
    project(7, 7)

    drain(len(pending))


def local(
    attn_heads, w_out, residual, gain_moe, router, route_ids,
    w_gate, w_up, w_down, bias, gain_next, w_query,
):
    width = residual.shape[1]
    vmem = pl.BlockSpec(memory_space=pltpu.VMEM)
    hbm = pl.BlockSpec(memory_space=pl.ANY)
    dma = pltpu.SemaphoreType.DMA
    scratch = [
        pltpu.VMEM((512, 256), BF), pltpu.VMEM((512, 256), BF), pltpu.VMEM((256, 2048), BF),
        pltpu.VMEM((2048, 768), BF), pltpu.VMEM((2048, 768), BF),
        pltpu.VMEM((768, 2048), BF), pltpu.VMEM((2048, 256), BF),
        pltpu.VMEM((TOK, width), BF), pltpu.VMEM((1, width), F32), pltpu.VMEM((64, width), BF),
        pltpu.VMEM((8, TOK), jnp.int32), pltpu.VMEM((1, 64), F32), pltpu.VMEM((1, width), F32),
        pltpu.VMEM((256, width), F32), pltpu.VMEM((256, width), BF), pltpu.VMEM((256, width), BF),
        pltpu.VMEM((2, 256, WIDE), BF), pltpu.VMEM((2, 256, WIDE), BF),
        pltpu.VMEM((2, 256, WIDE), BF), pltpu.VMEM((2, 256, WIDE), BF),
        pltpu.VMEM((256, width), BF), pltpu.VMEM((2, 512, WIDE), BF),
        pltpu.VMEM((TOK, width), F32), pltpu.VMEM((256, width), F32),
        pltpu.VMEM((256, 128), BF), pltpu.VMEM((256, 384), F32), pltpu.VMEM((384, 256), BF),
        pltpu.VMEM((256, 384), BF),
        pltpu.VMEM((384, width), BF), pltpu.VMEM((384, width), BF),
        pltpu.VMEM((384, width), BF), pltpu.VMEM((384, width), BF),
        pltpu.VMEM((8, 128), F32), pltpu.VMEM((64, 128), F32),
        pltpu.VMEM((96, 128), F32),
        dma((12,)), dma((8,)), dma((8,)),
        dma((32,)), dma((32,)), dma((32,)), dma((32,)),
        dma((16,)), dma((16,)), dma((32,)), dma((32,)),
        dma((32,)), dma((32,)), dma((8,)), dma((8,)),
        dma((24,)), dma((24,)), dma((24,)), dma((24,)),
        dma((8,)), dma((8,)), dma((12,)), dma((12,)),
    ]
    stream_out, query, new_bias = pl.pallas_call(
        kernel,
        out_shape=(
            jax.ShapeDtypeStruct((TOK, width), BF),
            jax.ShapeDtypeStruct((512, 256), BF),
            jax.ShapeDtypeStruct((1, 64), F32),
        ),
        in_specs=[hbm] * 12,
        out_specs=(vmem, vmem, vmem),
        scratch_shapes=scratch,
        compiler_params=pltpu.CompilerParams(
            collective_id=0, has_side_effects=True, vmem_limit_bytes=60 * 1024 * 1024
        ),
    )(
        attn_heads, w_out, residual, gain_moe.reshape(1, -1), router.T, route_ids.T,
        w_gate, w_up, w_down, bias.reshape(1, -1), gain_next.reshape(1, -1), w_query,
    )
    return stream_out, query, new_bias.reshape(-1)


def solution(mesh):
    in_specs = (
        P(("dp", "fold"), "tensor"),
        P("tensor", None),
        P(("dp", "fold", "tensor"), None),
        P(),
        P(),
        P(("dp", "fold", "tensor"), None),
        P(("fold", "tensor"), None, None),
        P(("fold", "tensor"), None, None),
        P(("fold", "tensor"), None, None),
        P(),
        P(),
        P(None, "tensor"),
    )
    out_specs = (P(("dp", "fold", "tensor"), None), P(("dp", "fold"), "tensor"), P())
    return jax.shard_map(local, mesh=mesh, in_specs=in_specs, out_specs=out_specs, check_vma=False)
```
